256 devices in a mesh: seq: 32 (over z, y), head: 4 (over x), rep: 2 (over core).
Axes of the slice: x: 4, y: 4, z: 8, core: 2. Of those that a mesh axis runs over, the one named last changes fastest.
Arguments:
- byte_states: bfloat16 [2, 8192, 3072], P('rep', 'seq', 'head'), may hold values from -6 to 6
- boundary: int32 [2, 8192], P('rep', 'seq'), may hold values from 0 to 1, as said below
- confidence: float32 [2, 8192], P('rep', 'seq'), may hold values from 0.5 to 1
- query_rows: bfloat16 [2, 2048, 3072], P('rep', 'seq', 'head'), may hold values from -50 to 50
- key_rows: bfloat16 [2, 2048, 3072], P('rep', 'seq', 'head'), may hold values from -6 to 6
- value_rows: bfloat16 [2, 2048, 3072], P('rep', 'seq', 'head'), may hold values from -6 to 6
- out_weight: bfloat16 [3072, 3072], P('seq', 'head'), may hold values from -0.109375 to 0.109375
- upstream: bfloat16 [2, 8192, 3072], P('rep', 'seq', 'head'), may hold values from -6 to 6
Outputs:
- byte_grad: bfloat16 [2, 8192, 3072], P('rep', 'seq', 'head')
- confidence_grad: float32 [2, 8192], P('rep', 'seq')
- query_grad: bfloat16 [2, 2048, 3072], P('rep', 'seq', 'head')
- key_grad: bfloat16 [2, 2048, 3072], P('rep', 'seq', 'head')
- value_grad: bfloat16 [2, 2048, 3072], P('rep', 'seq', 'head')
- weight_grad: float32 [3072, 3072], P('seq', 'head')
The draws below stay inside these ranges and needn't reach their ends.
Inputs may be any that keep to these rules, and one draw needn't show every extreme that they name: Each block of 256 bytes holds between 16 and 64 boundary bytes, in every window some block exactly 64; byte 0 of every window is a boundary byte, and the first byte of every other block is not.
All inputs are finite; a program needn't handle non-finite values.
Results may differ from the reference program's by a relative error of at most 0.04.
Values may be sent and summed in bfloat16 or wider, within the bound.
A program may use at most 128 MiB of HBM per device.

```python
import jax
import jax.numpy as jnp
from jax import lax

HEAD_DIM = 128
HEADS = 24
D = 3072
BYTE_DEV = 256
CAP = 64
WINDOWS = 2
BYTES = 8192
GROUPS = 2048


def draw_boundary(key, part):
    key = jax.random.fold_in(key, 11)
    block_total = BYTES // BYTE_DEV
    key_count = jax.random.fold_in(key, 0)
    key_full = jax.random.fold_in(key, 1)
    key_order = jax.random.fold_in(key, 3)
    counts = jax.random.randint(key_count, (WINDOWS, block_total), CAP // 4, CAP + 1)
    full_block = jax.random.randint(key_full, (WINDOWS, 1), 0, block_total)
    counts = jnp.where(jnp.arange(block_total)[None, :] == full_block, CAP, counts)
    first_mark = jnp.broadcast_to((jnp.arange(block_total) == 0).astype(jnp.int32)[None, :], (WINDOWS, block_total))
    order_keys = jax.random.split(key_order, WINDOWS * block_total)
    byte_order = jax.vmap(lambda single: jax.random.permutation(single, BYTE_DEV - 1))(order_keys)
    byte_order = byte_order.reshape(WINDOWS, block_total, BYTE_DEV - 1)
    remaining = (byte_order < (counts - first_mark)[:, :, None]).astype(jnp.int32)
    boundary_marks = jnp.concatenate([first_mark[:, :, None].astype(jnp.int32), remaining], axis=2)
    return boundary_marks.reshape(WINDOWS, BYTES).astype(jnp.int32)


def query_key_base(key):
    key_query = jax.random.fold_in(key, 101)
    key_keys = jax.random.fold_in(key, 202)
    array_shape = (WINDOWS, GROUPS, D)
    normal_query = jnp.clip(jax.random.normal(key_query, array_shape, jnp.float32), -6.0, 6.0)
    normal_keys = jnp.clip(jax.random.normal(key_keys, array_shape, jnp.float32), -6.0, 6.0)
    return (normal_query, normal_keys)


def draw_query_rows(key, part):
    normal_query, normal_keys = query_key_base(key)
    return normal_query.astype(jnp.bfloat16)


def draw_key_rows(key, part):
    normal_query, normal_keys = query_key_base(key)
    return normal_keys.astype(jnp.bfloat16)


def levels(own_key, shape, pieces, smallest, high):
    gain, own = 1.0, jax.random.fold_in(own_key, 6)
    for axis_at, shards_of in pieces:
        draws = jnp.exp(jax.random.uniform(jax.random.fold_in(own, axis_at), (shards_of,), jnp.float32, smallest / len(pieces), high / len(pieces)))
        gain = gain * jnp.repeat(draws, shape[axis_at] // shards_of).reshape([-1 if axis == axis_at else 1 for axis in range(len(shape))])
    return gain


def bell_draw(rng, extent, deviation, bound, pieces=(), kind=jnp.bfloat16):
    values = deviation * jax.random.normal(rng, extent, jnp.float32)
    if pieces:
        values = values * levels(rng, extent, pieces, -0.22, 0.18)
    return jnp.clip(values, -bound, bound).astype(kind)


def setup_inputs(seed: int = 0) -> dict:
    key_of = jax.random.split(jax.random.key(seed), 9)
    byte_states = bell_draw(key_of[0], (WINDOWS, BYTES, D), 1.0, 6.0, ((0, 2), (1, 32), (2, 4)))
    boundary = draw_boundary(jax.random.fold_in(key_of[8], 71), 0)
    confidence = jnp.clip(0.5 + 0.5 * jax.random.uniform(key_of[2], (WINDOWS, BYTES), jnp.float32) ** levels(key_of[2], (WINDOWS, BYTES), ((0, 2), (1, 32)), -0.2, 0.2), 0.5, 1.0)
    query_rows = draw_query_rows(jax.random.fold_in(key_of[8], 71), 0)
    key_rows = draw_key_rows(jax.random.fold_in(key_of[8], 71), 0)
    value_rows = bell_draw(key_of[5], (WINDOWS, GROUPS, D), 1.0, 6.0, ((0, 2), (1, 32), (2, 4)))
    out_weight = bell_draw(key_of[6], (D, D), D ** -0.5, 0.109375, ((0, 32), (1, 4)))
    upstream = bell_draw(key_of[7], (WINDOWS, BYTES, D), 1.0, 6.0, ((0, 2), (1, 32), (2, 4)))
    return {"byte_states": byte_states, "boundary": boundary, "confidence": confidence, "query_rows": query_rows, "key_rows": key_rows, "value_rows": value_rows, "out_weight": out_weight, "upstream": upstream}


far_position = 1073741824


def group_layout(boundary):
    block_total = BYTES // BYTE_DEV
    blocks = boundary.reshape(block_total, BYTE_DEV)
    byte_rank = (jnp.cumsum(blocks, axis=1) - 1).astype(jnp.int32)
    counts = jnp.sum(blocks, axis=1).astype(jnp.int32)
    offsets = (jnp.cumsum(counts) - counts).astype(jnp.int32)
    block_ids = jnp.arange(block_total, dtype=jnp.int32)[:, None]
    earlier = jnp.concatenate([jnp.zeros((1,), jnp.int32), counts[:-1]])
    slot_of_byte = jnp.where(byte_rank >= 0, block_ids * CAP + byte_rank, (block_ids - 1) * CAP + earlier[:, None] - 1)
    slot_index = jnp.arange(CAP, dtype=jnp.int32)[None, :]
    is_live = slot_index < counts[:, None]
    query_pos = jnp.where(is_live, offsets[:, None] + slot_index, far_position).reshape(GROUPS)
    key_pos = jnp.where(is_live, offsets[:, None] + slot_index, far_position + 1).reshape(GROUPS)
    return slot_of_byte.reshape(BYTES).astype(jnp.int32), query_pos.astype(jnp.int32), key_pos.astype(jnp.int32)


def per_head(array_in):
    return array_in.reshape(GROUPS, HEADS, HEAD_DIM).transpose(1, 0, 2)


def from_heads(array_in):
    return array_in.transpose(1, 0, 2).reshape(GROUPS, D)


def one_window(states, boundary, confidence, queries, keys_in, values, weight, upstream):
    slot_of_byte, query_pos, key_pos = group_layout(boundary)
    starts = boundary == 1
    target = jnp.where(starts, slot_of_byte, GROUPS)
    group_rows = jnp.zeros((GROUPS, D), jnp.float32).at[target].set(states.astype(jnp.float32), mode="drop")
    allowed = key_pos[None, :] <= query_pos[:, None]
    score_scale = HEAD_DIM ** -0.5
    head_query, head_key, head_value = per_head(queries), per_head(keys_in), per_head(values)

    def forward_head(operands):
        one_query, one_key, one_value = operands
        scores = jnp.where(allowed, jnp.dot(one_query, one_key.T, preferred_element_type=jnp.float32) * score_scale, -jnp.inf)
        row_top = jnp.max(scores, axis=1)
        attention = jnp.exp(scores - row_top[:, None])
        row_total = jnp.sum(attention, axis=1)
        result = jnp.dot(attention.astype(jnp.bfloat16), one_value, preferred_element_type=jnp.float32) / row_total[:, None]
        return result.astype(jnp.bfloat16), row_top + jnp.log(row_total)

    head_out, log_total = lax.map(forward_head, (head_query, head_key, head_value))
    attended = from_heads(head_out)
    group_out = (group_rows + jnp.dot(attended, weight.T, preferred_element_type=jnp.float32)).astype(jnp.bfloat16)
    upstream_wide = upstream.astype(jnp.float32)
    weighted = confidence[:, None] * upstream_wide
    group_grad = jax.ops.segment_sum(weighted, slot_of_byte, num_segments=GROUPS)
    conf_grad = jnp.sum(upstream_wide * group_out[slot_of_byte].astype(jnp.float32), axis=1)
    byte_grad = (upstream_wide + jnp.where(starts[:, None], group_grad[slot_of_byte], 0.0)).astype(jnp.bfloat16)
    grad_round = group_grad.astype(jnp.bfloat16)
    out_grad = jnp.dot(grad_round, weight, preferred_element_type=jnp.float32).astype(jnp.bfloat16)
    weight_grad = jnp.dot(grad_round.T, attended, preferred_element_type=jnp.float32)
    head_grad = per_head(out_grad)
    row_dot = jnp.sum(head_grad.astype(jnp.float32) * head_out.astype(jnp.float32), axis=2)

    def backward_head(operands):
        one_query, one_key, one_value, one_grad, one_total, one_dot = operands
        scores = jnp.where(allowed, jnp.dot(one_query, one_key.T, preferred_element_type=jnp.float32) * score_scale, -jnp.inf)
        back_probs = jnp.exp(scores - one_total[:, None])
        grad_value = jnp.dot(back_probs.astype(jnp.bfloat16).T, one_grad, preferred_element_type=jnp.float32)
        flow_grad = jnp.dot(one_grad, one_value.T, preferred_element_type=jnp.float32)
        dscore = (back_probs * (flow_grad - one_dot[:, None])).astype(jnp.bfloat16)
        grad_query = jnp.dot(dscore, one_key, preferred_element_type=jnp.float32) * score_scale
        grad_key = jnp.dot(dscore.T, one_query, preferred_element_type=jnp.float32) * score_scale
        return grad_query.astype(jnp.bfloat16), grad_key.astype(jnp.bfloat16), grad_value.astype(jnp.bfloat16)

    grad_q, grad_k, grad_v = lax.map(backward_head, (head_query, head_key, head_value, head_grad, log_total, row_dot))
    return byte_grad, conf_grad, from_heads(grad_q), from_heads(grad_k), from_heads(grad_v), weight_grad


def reference(byte_states, boundary, confidence, query_rows, key_rows, value_rows, out_weight, upstream):
    results = [one_window(byte_states[index], boundary[index], confidence[index], query_rows[index], key_rows[index], value_rows[index], out_weight, upstream[index]) for index in range(WINDOWS)]
    byte_grad = jnp.stack([entry[0] for entry in results])
    confidence_grad = jnp.stack([entry[1] for entry in results])
    query_grad = jnp.stack([entry[2] for entry in results])
    key_grad = jnp.stack([entry[3] for entry in results])
    value_grad = jnp.stack([entry[4] for entry in results])
    weight_grad = results[0][5]
    for entry in results[1:]:
        weight_grad = weight_grad + entry[5]
    return byte_grad, confidence_grad, query_grad, key_grad, value_grad, weight_grad
```

```python
import jax
import jax.numpy as jnp
from jax import lax
from jax.experimental import pallas as pl
from jax.experimental.pallas import tpu as pltpu
from jax.sharding import PartitionSpec as P

MESH = pl.DeviceIdType.MESH
F32, BF16 = jnp.float32, jnp.bfloat16

HEAD_DIM = 128
NS = 32
NH = 6
D = 768
CAP = 64
NB = 256
SCALE = HEAD_DIM ** -0.5
SCALE_LOG2E = SCALE * 1.4426950408889634
FAR_QUERY = 4096.0
FAR_KEY = 8192.0


def att_seq(h, w):
    return lax.div((2 * h + w) * 8, 3)


def nt(a, b):
    return lax.dot_general(a, b, (((1,), (1,)), ((), ())), preferred_element_type=F32)


def nn(a, b):
    return jnp.dot(a, b, preferred_element_type=F32)


def kernel(
    states, starts, conf, q_in, k_in, v_in, w_in, up,
    byte_grad, conf_grad, dq_out, dk_out, dv_out, wg_out,
    stage, kv, qb, wq, gext, spill_in, g_bf, gq, dop, dob,
    kt, vt, kkb, probs, inv, a_out, ab, pp, pr, wgp, wgr, wsum, wsib,
    lrow, prow, cpart, call, dqb, acc, sib, dkf, sel_s, grows,
    kv_send, kv_recv, q_send, q_recv, w_send, w_recv, sp_send, sp_recv, g_send, g_recv,
    do_send, do_recv, a_send, a_recv, p_send, p_recv, wg_send, wg_recv, ws_send, ws_recv,
    lr_send, lr_recv, c_send, c_recv, dq_send, dq_recv, dk_send, dk_recv, dv_send, dv_recv,
    ex_send, ex_recv,
):
    s = lax.axis_index("seq")
    x = lax.axis_index("head")
    r = lax.axis_index("rep")
    q = lax.div(s, 8)
    m = lax.rem(s, 8)
    half = lax.div(q, 2)
    sub = lax.rem(q, 2)
    att = lax.div(3 * s + 7, 8)
    is_att = jnp.logical_and(lax.div(att * 8, 3) == s, att < 12)
    att_h = lax.div(att, 2)
    att_w = lax.rem(att, 2)

    def same(t):
        return jnp.logical_and(jnp.logical_and(t[0] == s, t[1] == x), t[2] == r)

    def send(src, dst, ssem, rsem, t):
        mine = same(t)

        @pl.when(jnp.logical_not(mine))
        def _():
            pltpu.make_async_remote_copy(src, dst, ssem, rsem, device_id=t, device_id_type=MESH).start()

        @pl.when(mine)
        def _():
            pltpu.make_async_copy(src, dst, rsem).start()

    def sent(src, dst, ssem, rsem, t):
        @pl.when(jnp.logical_not(same(t)))
        def _():
            pltpu.make_async_remote_copy(src, dst, ssem, rsem, device_id=t, device_id_type=MESH).wait_send()

    def landed(ref, rsem):
        pltpu.make_async_copy(ref, ref, rsem).wait()

    def lanes(h):
        return pl.ds(h * HEAD_DIM if isinstance(h, int) else pl.multiple_of(h * HEAD_DIM, HEAD_DIM), HEAD_DIM)

    def kv_flow(op):
        for h in range(NH):
            for c in range(2):
                op(stage.at[h], kv.at[s], kv_send.at[2 * h + c], kv_recv, (att_seq(h, r), x, c))

    def q_flow(op):
        for h in range(NH):
            op(q_in.at[0, :, lanes(h)], qb.at[m, sub], q_send.at[h], q_recv, (att_seq(h, r), x, half))

    def w_flow(op):
        for i in range(1, 8):
            op(w_in, wq.at[m], w_send.at[i - 1], w_recv, (8 * q + lax.rem(m + i, 8), x, r))

    def g_flow(op):
        for i in range(4):
            op(g_bf, gq.at[q], g_send.at[i], g_recv, (8 * x + m, i, r))

    def do_flow(op):
        for h in range(NH):
            for c in range(2):
                op(dop.at[pl.ds(2 * c, 2), :, lanes(h)], dob.at[q, m], do_send.at[2 * h + c], do_recv,
                   (att_seq(h, r), x, c))

    def a_flow(op, mm):
        for i in range(4):
            op(a_out.at[mm], ab.at[pl.ds(2 * r, 2), :, lanes(att_h)], a_send.at[mm * 4 + i], a_recv,
               (8 * i + mm, x, att_w))

    def p_flow(op):
        for k in range(4):
            op(pp.at[k], pr.at[x], p_send.at[k], p_recv, (8 * k + m, q, r))

    def wg_flow(op):
        for i in range(1, 8):
            t = lax.rem(m + i, 8)
            op(wgp.at[t], wgr.at[m], wg_send.at[i - 1], wg_recv, (8 * q + t, x, r))

    def c_flow(op):
        for i in range(1, 4):
            op(cpart, call.at[x], c_send.at[i - 1], c_recv, (s, lax.rem(x + i, 4), r))

    def dq_flow(op, mm):
        for k in range(2):
            op(dqb.at[mm, k], dq_out.at[0, :, lanes(att_h)], dq_send.at[mm * 2 + k], dq_recv,
               (8 * (2 * r + k) + mm, x, att_w))

    def dkv_flow(op, j):
        op(dkf.at[0, j], dk_out.at[0, :, lanes(att_h)], dk_send.at[j], dk_recv, (16 * r + j, x, att_w))
        op(dkf.at[1, j], dv_out.at[0, :, lanes(att_h)], dv_send.at[j], dv_recv, (16 * r + j, x, att_w))

    def remote(src, dst, ssem, rsem, t):
        return pltpu.make_async_remote_copy(src, dst, ssem, rsem, device_id=t, device_id_type=MESH)

    spill_copy = remote(gext.at[pl.ds(64, 8)], spill_in, sp_send, sp_recv, (s - 1, x, r))
    row_copy = remote(lrow, prow, lr_send, lr_recv, (s + 1, x, r))
    sib_id = (s, x, 1 - r)
    wsum_copy = remote(wsum, wsib, ws_send, ws_recv, sib_id)
    ex_copy = remote(acc.at[1 - r], sib, ex_send, ex_recv, sib_id)

    barrier = pltpu.get_barrier_semaphore()

    def greet(t):
        @pl.when(jnp.logical_not(same(t)))
        def _():
            pl.semaphore_signal(barrier, inc=1, device_id=t, device_id_type=MESH)

    for h in range(NH):
        for c in range(2):
            greet((att_seq(h, r), x, c))
    for i in range(1, 8):
        greet((8 * q + lax.rem(m + i, 8), x, r))
    for k in range(4):
        for i in range(4):
            greet((8 * k + m, i, r))
    greet(sib_id)

    @pl.when(s > 0)
    def _():
        greet((s - 1, x, r))

    @pl.when(s < NS - 1)
    def _():
        greet((s + 1, x, r))

    @pl.when(is_att)
    def _():
        def one(j, _):
            greet((j, x, att_w))
            return 0

        lax.fori_loop(0, NS, one, 0)

    start_row = starts[...].astype(F32)
    before = lax.broadcasted_iota(jnp.int32, (NB, NB), 0) <= lax.broadcasted_iota(jnp.int32, (NB, NB), 1)
    tri = jnp.where(before, 1.0, 0.0).astype(BF16)
    rank = nn(jnp.broadcast_to(start_row, (16, NB)).astype(BF16), tri)[0:1] - 1.0
    count = jnp.sum(start_row, axis=1, keepdims=True)
    for h in range(NH):
        cols = slice(h * HEAD_DIM, (h + 1) * HEAD_DIM)
        stage[h, 0:64] = k_in[0, :, cols]
        stage[h, 64:128] = v_in[0, :, cols]
        stage[h, 128:144] = jnp.broadcast_to(count, (16, HEAD_DIM)).astype(BF16)
    slot80 = lax.broadcasted_iota(jnp.int32, (80, NB), 0).astype(F32)
    want = jnp.where(slot80 < 64.0, slot80, jnp.where(slot80 == 64.0, -1.0, -2.0))
    sel = jnp.where(jnp.broadcast_to(rank, (80, NB)) == want, 1.0, 0.0)
    sel_s[...] = sel

    partners = (
        12 + 7 + 15 + 1
        + jnp.where(s > 0, 1, 0) + jnp.where(s < NS - 1, 1, 0)
        + jnp.where(is_att, jnp.where(att_w == r, 30, 32), 0)
    )
    pl.semaphore_wait(barrier, partners)

    kv_flow(send)
    q_flow(send)
    w_flow(lambda *a: remote(*a).start())
    wq[m] = w_in[...]

    weight = sel * conf[...]
    w_hi = weight.astype(BF16)
    w_lo = (weight - w_hi.astype(F32)).astype(BF16)
    upstream = up[0]
    gext[...] = nn(w_hi, upstream) + nn(w_lo, upstream)

    @pl.when(s > 0)
    def _():
        spill_copy.start()

    @pl.when(s == NS - 1)
    def _():
        spill_in[...] = jnp.zeros_like(spill_in)

    @pl.when(s == 0)
    def _():
        prow[...] = jnp.zeros_like(prow)

    picked = sel[0:64] * start_row
    picked_t = picked.T.astype(BF16)
    grows[...] = nn(picked.astype(BF16), states[0])

    @pl.when(s < NS - 1)
    def _():
        spill_copy.wait_recv()

    last = lax.broadcasted_iota(jnp.int32, (64, D), 0).astype(F32) == count - 1.0
    group_grad = gext[0:64] + jnp.where(last, spill_in[0:1], 0.0)
    g_hi = group_grad.astype(BF16)
    g_bf[...] = g_hi
    g_flow(send)
    g_lo = (group_grad - g_hi.astype(F32)).astype(BF16)
    byte_grad[0] = (upstream.astype(F32) + nn(picked_t, g_hi) + nn(picked_t, g_lo)).astype(BF16)

    @pl.when(is_att)
    def _():
        landed(kv, kv_recv)
        landed(qb, q_recv)
        kt[...] = kv[:, 0:64, :].reshape(2048, HEAD_DIM).T
        vt[...] = kv[:, 64:128, :].reshape(2048, HEAD_DIM).T
        lane = lax.broadcasted_iota(jnp.int32, (1, 128), 1).astype(F32)
        for p in range(16):
            c0 = kv[2 * p, 128:144, :].astype(F32)[0:1]
            c1 = kv[2 * p + 1, 128:144, :].astype(F32)[0:1]
            live = jnp.where(lane < 64.0, jnp.where(lane < c0, 1.0, 0.0), jnp.where(lane - 64.0 < c1, 1.0, 0.0))
            row = jnp.where(live > 0.0, lane + 128.0 * p, FAR_KEY)
            kkb[:, p * 128:(p + 1) * 128] = jnp.broadcast_to(row, (8, 128))

        def forward(i, _):
            queries = qb[pl.ds(2 * i, 2)].reshape(256, HEAD_DIM)
            slot = lax.broadcasted_iota(jnp.int32, (64, 128), 0).astype(F32)
            places = []
            for mm in range(2):
                for k in range(2):
                    block = 8 * (2 * r + k) + 2 * i + mm
                    cnt = kv[block, 128:144, :].astype(F32)[0:1]
                    base = (block * 64).astype(F32)
                    places.append(jnp.where(slot < cnt, slot + base, FAR_QUERY))
            place = jnp.concatenate(places, axis=0)
            place = jnp.concatenate([place] * 16, axis=1)
            scores = nn(queries, kt[...])
            scores = jnp.where(jnp.broadcast_to(kkb[0:1], (256, 2048)) <= place, scores, -jnp.inf)
            top = jnp.max(scores, axis=1, keepdims=True)
            attention = jnp.exp2((scores - top) * SCALE_LOG2E)
            total = jnp.sum(attention, axis=1, keepdims=True)
            rounded = attention.astype(BF16)
            probs[i] = rounded
            inverse = 1.0 / total
            inv[i] = jnp.broadcast_to(inverse, (256, HEAD_DIM))
            out = nn(rounded, kv[:, 64:128, :].reshape(2048, HEAD_DIM)) * inverse
            a_out[pl.ds(2 * i, 2)] = out.astype(BF16).reshape(2, 2, 64, HEAD_DIM)
            a_flow(send, 2 * i)
            a_flow(send, 2 * i + 1)
            return 0

        lax.fori_loop(0, 4, forward, 0)

    landed(wq.at[pl.ds(0, 7)], w_recv)
    landed(gq, g_recv)
    g_all = gq[...].reshape(256, D)
    w_all = wq[...].reshape(D, D)
    dop[...] = nn(g_all, w_all).astype(BF16).reshape(4, 64, D)
    do_flow(send)

    landed(ab, a_recv)
    a_all = ab[...].reshape(256, D)
    pp[...] = nt(a_all, w_all).astype(BF16).reshape(4, 64, D)
    p_flow(send)
    wgp[...] = nn(g_all.T, a_all).astype(BF16).reshape(8, 96, D)
    wg_flow(lambda *a: remote(*a).start())

    @pl.when(is_att)
    def _():
        landed(dob, do_recv)
        acc[...] = jnp.zeros_like(acc)

        def backward(i, _):
            queries = qb[pl.ds(2 * i, 2)].reshape(256, HEAD_DIM)
            grad = dob[0, pl.ds(2 * i, 2)].astype(F32)
            for j in range(1, 4):
                grad = grad + dob[j, pl.ds(2 * i, 2)].astype(F32)
            grad = grad.reshape(256, HEAD_DIM).astype(BF16).astype(F32)
            grad = (grad * inv[i]).astype(BF16)
            attended = a_out[pl.ds(2 * i, 2)].reshape(256, HEAD_DIM)
            dots = jnp.sum(grad.astype(F32) * attended.astype(F32), axis=1, keepdims=True)
            flow = nn(grad, vt[...])
            weights = probs[i]
            dscore = (weights.astype(F32) * (flow - dots)).astype(BF16)
            dq = nn(dscore, kv[:, 0:64, :].reshape(2048, HEAD_DIM)) * SCALE
            dqb[pl.ds(2 * i, 2)] = dq.astype(BF16).reshape(2, 2, 64, HEAD_DIM)
            dq_flow(send, 2 * i)
            dq_flow(send, 2 * i + 1)
            dk = nn(queries.T, dscore)
            dv = nn(grad.T, weights)
            for c in range(2):
                cols = slice(1024 * c, 1024 * (c + 1))
                acc[c, 0] += dk[:, cols]
                acc[c, 1] += dv[:, cols]
            return 0

        lax.fori_loop(0, 4, backward, 0)
        ex_copy.start()
        ex_copy.wait_recv()
        dkf[0] = ((acc[r, 0] + sib[0]) * SCALE).T.astype(BF16).reshape(16, 64, HEAD_DIM)
        dkf[1] = (acc[r, 1] + sib[1]).T.astype(BF16).reshape(16, 64, HEAD_DIM)

        def out(j, _):
            dkv_flow(send, j)
            return 0

        lax.fori_loop(0, 16, out, 0)

    landed(pr, p_recv)
    total = grows[...]
    for i in range(4):
        total = total + pr[i].astype(F32)
    group_out = total.astype(BF16)
    lrow[...] = jnp.broadcast_to(
        jnp.sum(jnp.where(last, group_out.astype(F32), 0.0), axis=0, keepdims=True), (16, D)
    ).astype(BF16)

    @pl.when(s < NS - 1)
    def _():
        row_copy.start()

    landed(wgr.at[pl.ds(0, 7)], wg_recv)
    wgr[m] = wgp[m]
    total_w = wgr[0].astype(F32)
    for i in range(1, 8):
        total_w = total_w + wgr[i].astype(F32)
    wsum[...] = total_w
    wsum_copy.start()

    @pl.when(s > 0)
    def _():
        row_copy.wait_recv()

    rows = jnp.concatenate([group_out, prow[...]], axis=0)
    cross = nt(rows, up[0])
    part = jnp.sum(sel_s[...] * cross, axis=0, keepdims=True)
    cpart[...] = jnp.broadcast_to(part, (8, NB))
    call[x] = cpart[...]
    c_flow(lambda *a: remote(*a).start())

    wsum_copy.wait_recv()
    wg_out[...] = wsum[...] + wsib[...]
    landed(call.at[pl.ds(0, 3)], c_recv)
    conf_grad[...] = (call[0] + call[1] + call[2] + call[3])[0:1]

    kv_flow(sent)
    q_flow(sent)
    w_flow(sent)
    g_flow(sent)
    do_flow(sent)
    p_flow(sent)
    wg_flow(sent)
    c_flow(sent)
    wsum_copy.wait_send()

    @pl.when(s > 0)
    def _():
        spill_copy.wait_send()

    @pl.when(s < NS - 1)
    def _():
        row_copy.wait_send()

    @pl.when(is_att)
    def _():
        ex_copy.wait_send()

        def one(j, _):
            a_flow(sent, j)
            dq_flow(sent, j)
            return 0

        lax.fori_loop(0, 8, one, 0)

        def two(j, _):
            dkv_flow(sent, j)
            return 0

        lax.fori_loop(0, 16, two, 0)

    landed(dq_out, dq_recv)
    landed(dk_out, dk_recv)
    landed(dv_out, dv_recv)


def local(byte_states, boundary, confidence, query_rows, key_rows, value_rows, out_weight, upstream):
    vmem = pl.BlockSpec(memory_space=pltpu.VMEM)
    dma = pltpu.SemaphoreType.DMA
    rows = jax.ShapeDtypeStruct((1, CAP, D), BF16)
    return pl.pallas_call(
        kernel,
        out_shape=(
            jax.ShapeDtypeStruct((1, NB, D), BF16),
            jax.ShapeDtypeStruct((1, NB), F32),
            rows, rows, rows,
            jax.ShapeDtypeStruct((96, D), F32),
        ),
        in_specs=[vmem] * 8,
        out_specs=(vmem,) * 6,
        scratch_shapes=[
            pltpu.VMEM((NH, 144, 128), BF16),
            pltpu.VMEM((NS, 144, 128), BF16),
            pltpu.VMEM((8, 2, 64, 128), BF16),
            pltpu.VMEM((8, 96, D), BF16),
            pltpu.VMEM((80, D), F32),
            pltpu.VMEM((8, D), F32),
            pltpu.VMEM((64, D), BF16),
            pltpu.VMEM((4, 64, D), BF16),
            pltpu.VMEM((4, 64, D), BF16),
            pltpu.VMEM((4, 8, 2, 64, 128), BF16),
            pltpu.VMEM((128, 2048), BF16),
            pltpu.VMEM((128, 2048), BF16),
            pltpu.VMEM((8, 2048), F32),
            pltpu.VMEM((4, 256, 2048), BF16),
            pltpu.VMEM((4, 256, 128), F32),
            pltpu.VMEM((8, 2, 64, 128), BF16),
            pltpu.VMEM((4, 64, D), BF16),
            pltpu.VMEM((4, 64, D), BF16),
            pltpu.VMEM((4, 64, D), BF16),
            pltpu.VMEM((8, 96, D), BF16),
            pltpu.VMEM((8, 96, D), BF16),
            pltpu.VMEM((96, D), F32),
            pltpu.VMEM((96, D), F32),
            pltpu.VMEM((16, D), BF16),
            pltpu.VMEM((16, D), BF16),
            pltpu.VMEM((8, NB), F32),
            pltpu.VMEM((4, 8, NB), F32),
            pltpu.VMEM((8, 2, 64, 128), BF16),
            pltpu.VMEM((2, 2, 128, 1024), F32),
            pltpu.VMEM((2, 128, 1024), F32),
            pltpu.VMEM((2, 16, 64, 128), BF16),
            pltpu.VMEM((80, NB), F32),
            pltpu.VMEM((64, D), F32),
            dma((12,)), dma,
            dma((6,)), dma,
            dma((7,)), dma,
            dma, dma,
            dma((4,)), dma,
            dma((12,)), dma,
            dma((32,)), dma,
            dma((4,)), dma,
            dma((7,)), dma,
            dma, dma,
            dma, dma,
            dma((3,)), dma,
            dma((16,)), dma,
            dma((16,)), dma,
            dma((16,)), dma,
            dma, dma,
        ],
        compiler_params=pltpu.CompilerParams(
            collective_id=0, has_side_effects=True, vmem_limit_bytes=56 * 1024 * 1024
        ),
        cost_estimate=pl.CostEstimate(flops=8_000_000_000, bytes_accessed=20_000_000, transcendentals=3_000_000),
    )(byte_states, boundary, confidence, query_rows, key_rows, value_rows, out_weight, upstream)


def solution(mesh):
    split = P("rep", "seq", "head")
    bytes_ = P("rep", "seq")
    return jax.shard_map(
        local,
        mesh=mesh,
        in_specs=(split, bytes_, bytes_, split, split, split, P("seq", "head"), split),
        out_specs=(split, bytes_, split, split, split, P("seq", "head")),
        check_vma=False,
    )
```

```python
import jax
import jax.numpy as jnp
from jax import lax
from jax.experimental import pallas as pl
from jax.experimental.pallas import tpu as pltpu
from jax.sharding import PartitionSpec as P

MESH = pl.DeviceIdType.MESH
F32, BF16 = jnp.float32, jnp.bfloat16

HEAD_DIM = 128
NS = 32
NH = 6
D = 768
CAP = 64
NB = 256
SCALE = HEAD_DIM ** -0.5
SCALE_LOG2E = SCALE * 1.4426950408889634
FAR_QUERY = 4096.0
FAR_KEY = 8192.0


def att_seq(h, w):
    return lax.div((2 * h + w) * 8, 3)


def nt(a, b):
    return lax.dot_general(a, b, (((1,), (1,)), ((), ())), preferred_element_type=F32)


def nn(a, b):
    return jnp.dot(a, b, preferred_element_type=F32)


def kernel(
    states, starts, conf, q_in, k_in, v_in, w_in, up,
    byte_grad, conf_grad, dq_out, dk_out, dv_out, wg_out,
    stage, kv, wq, gext, spill_in, g_bf, gq, dop, dob,
    kt, vt, kkb, probs, inv, a_out, ab, pp, p1, ps, pr, wgp, wgs, wg0, wh, wg1, wt, wg2, wsum,
    lrow, prow, cpart, call, dqb, acc, sib, dkf, sel_s, grows,
    kv_send, kv_recv, fw_send, fw_recv, wa_send, wa_recv, wb_send, wb_recv, wc_send, wc_recv, wd_send, wd_recv,
    sp_send, sp_recv, g_send, g_recv, gx_send, gx_recv,
    do_send, do_recv, a_send, a_recv, px_send, px_recv, p_send, p_recv,
    w0_send, w0_recv, w1_send, w1_recv, w2_send, w2_recv, ws_send, ws_recv,
    lr_send, lr_recv, c_send, c_recv, dq_send, dq_recv, dk_send, dk_recv, dv_send, dv_recv,
    ex_send, ex_recv,
):
    s = lax.axis_index("seq")
    x = lax.axis_index("head")
    r = lax.axis_index("rep")
    q = lax.div(s, 8)
    m = lax.rem(s, 8)
    zp = lax.div(m, 4)
    y = lax.rem(m, 4)
    half = lax.div(q, 2)
    att = lax.div(3 * s + 7, 8)
    is_att = jnp.logical_and(lax.div(att * 8, 3) == s, att < 12)
    att_h = lax.div(att, 2)
    att_w = lax.rem(att, 2)

    def same(t):
        return jnp.logical_and(jnp.logical_and(t[0] == s, t[1] == x), t[2] == r)

    def send(src, dst, ssem, rsem, t):
        mine = same(t)

        @pl.when(jnp.logical_not(mine))
        def _():
            pltpu.make_async_remote_copy(src, dst, ssem, rsem, device_id=t, device_id_type=MESH).start()

        @pl.when(mine)
        def _():
            pltpu.make_async_copy(src, dst, rsem).start()

    def sent(src, dst, ssem, rsem, t):
        @pl.when(jnp.logical_not(same(t)))
        def _():
            pltpu.make_async_remote_copy(src, dst, ssem, rsem, device_id=t, device_id_type=MESH).wait_send()

    def landed(ref, rsem):
        pltpu.make_async_copy(ref, ref, rsem).wait()

    def remote(src, dst, ssem, rsem, t):
        return pltpu.make_async_remote_copy(src, dst, ssem, rsem, device_id=t, device_id_type=MESH)

    def start(*a):
        remote(*a).start()

    def finish(*a):
        remote(*a).wait_send()

    def lanes(h):
        return pl.ds(h * HEAD_DIM if isinstance(h, int) else pl.multiple_of(h * HEAD_DIM, HEAD_DIM), HEAD_DIM)

    mine48 = pl.ds(pl.multiple_of(48 * r, 16), 48)
    z_peer = (s + 4 - 8 * zp, x, r)
    sib_id = (s, x, 1 - r)

    def y_peer(i):
        return (s - y + lax.rem(y + i, 4), x, r)

    def x_peer(i):
        return (s, lax.rem(x + i, 4), r)

    def kv_flow(op):
        for h in range(NH):
            op(stage.at[h], kv.at[s], kv_send.at[h], kv_recv, (att_seq(h, r), x, half))

    def wa_flow(op):
        op(w_in.at[mine48], wq.at[zp, y, mine48], wa_send, wa_recv, z_peer)

    def wb_flow(op):
        for i in range(1, 4):
            op(w_in.at[mine48], wq.at[zp, y, mine48], wb_send.at[i - 1], wb_recv, y_peer(i))

    def wc_flow(op):
        for i in range(1, 4):
            op(wq.at[1 - zp, y, mine48], wq.at[1 - zp, y, mine48], wc_send.at[i - 1], wc_recv, y_peer(i))

    def wd_flow(op):
        op(wq.at[:, :, mine48], wq.at[:, :, mine48], wd_send, wd_recv, sib_id)

    turned = (8 * x + m, q, r)

    def g_flow(op):
        op(g_bf, gq.at[q], g_send, g_recv, turned)

    def gx_flow(op):
        for i in range(1, 4):
            op(gq.at[x], gq.at[x], gx_send.at[i - 1], gx_recv, x_peer(i))

    def do_flow(op):
        for h in range(NH):
            for c in range(2):
                op(dop.at[pl.ds(2 * c, 2), :, lanes(h)], dob.at[q, m], do_send.at[2 * h + c], do_recv,
                   (att_seq(h, r), x, c))

    def a_flow(op, mm):
        for i in range(4):
            op(a_out.at[mm], ab.at[pl.ds(2 * r, 2), :, lanes(att_h)], a_send.at[mm * 4 + i], a_recv,
               (8 * i + mm, x, att_w))

    def px_flow(op):
        for i in range(1, 4):
            op(pp.at[lax.rem(x + i, 4)], p1.at[x], px_send.at[i - 1], px_recv, x_peer(i))

    def p_flow(op):
        op(ps, pr, p_send, p_recv, turned)

    def w0_flow(op):
        op(wgs, wg0, w0_send, w0_recv, sib_id)

    def w1_flow(op):
        for i in range(1, 4):
            op(wh.at[:, lax.rem(y + i, 4)], wg1.at[y], w1_send.at[i - 1], w1_recv, y_peer(i))

    def w2_flow(op):
        op(wt.at[1 - zp], wg2, w2_send, w2_recv, z_peer)

    def ws_flow(op):
        op(wsum, wg_out.at[mine48], ws_send, ws_recv, sib_id)

    def c_flow(op):
        for i in range(1, 4):
            op(cpart, call.at[x], c_send.at[i - 1], c_recv, x_peer(i))

    def dq_flow(op, mm):
        for k in range(2):
            op(dqb.at[mm, k], dq_out.at[0, :, lanes(att_h)], dq_send.at[mm * 2 + k], dq_recv,
               (8 * (2 * r + k) + mm, x, att_w))

    def dkv_flow(op, j):
        op(dkf.at[0, j], dk_out.at[0, :, lanes(att_h)], dk_send.at[j], dk_recv, (16 * r + j, x, att_w))
        op(dkf.at[1, j], dv_out.at[0, :, lanes(att_h)], dv_send.at[j], dv_recv, (16 * r + j, x, att_w))

    def fw_flow(op):
        part = kv.at[pl.ds(16 * r, 16), pl.ds(0, 144)]
        op(part, part, fw_send, fw_recv, sib_id)

    spill_copy = remote(gext.at[pl.ds(64, 8)], spill_in, sp_send, sp_recv, (s - 1, x, r))
    row_copy = remote(lrow, prow, lr_send, lr_recv, (s + 1, x, r))
    ex_copy = remote(acc.at[1 - r], sib, ex_send, ex_recv, sib_id)

    barrier = pltpu.get_barrier_semaphore()

    def greet(t):
        @pl.when(jnp.logical_not(same(t)))
        def _():
            pl.semaphore_signal(barrier, inc=1, device_id=t, device_id_type=MESH)

    for h in range(NH):
        for c in range(2):
            greet((att_seq(h, r), x, c))
    for i in range(1, 4):
        greet(y_peer(i))
        greet(x_peer(i))
    greet(z_peer)
    greet(turned)
    greet(sib_id)

    @pl.when(s > 0)
    def _():
        greet((s - 1, x, r))

    @pl.when(s < NS - 1)
    def _():
        greet((s + 1, x, r))

    @pl.when(is_att)
    def _():
        def one(j, _):
            greet((j, x, att_w))
            return 0

        lax.fori_loop(0, NS, one, 0)

    start_row = starts[...].astype(F32)
    before = lax.broadcasted_iota(jnp.int32, (NB, NB), 0) <= lax.broadcasted_iota(jnp.int32, (NB, NB), 1)
    tri = jnp.where(before, 1.0, 0.0).astype(BF16)
    rank = nn(jnp.broadcast_to(start_row, (16, NB)).astype(BF16), tri)[0:1] - 1.0
    count = jnp.sum(start_row, axis=1, keepdims=True)
    slot80 = lax.broadcasted_iota(jnp.int32, (80, NB), 0).astype(F32)
    want = jnp.where(slot80 < 64.0, slot80, jnp.where(slot80 == 64.0, -1.0, -2.0))
    sel = jnp.where(jnp.broadcast_to(rank, (80, NB)) == want, 1.0, 0.0)
    sel_s[...] = sel
    weight = sel * conf[...]
    w_hi = weight.astype(BF16)
    w_lo = (weight - w_hi.astype(F32)).astype(BF16)
    upstream = up[0]
    gext[...] = nn(w_hi, upstream) + nn(w_lo, upstream)
    for h in range(NH):
        cols = slice(h * HEAD_DIM, (h + 1) * HEAD_DIM)
        stage[h, 0:64] = k_in[0, :, cols]
        stage[h, 64:128] = v_in[0, :, cols]
        stage[h, 128:144] = jnp.broadcast_to(count, (16, HEAD_DIM)).astype(BF16)
        stage[h, 144:208] = q_in[0, :, cols]
    picked = sel[0:64] * start_row
    picked_t = picked.T.astype(BF16)
    grows[...] = nn(picked.astype(BF16), states[0])
    wq[zp, y, mine48] = w_in[mine48]

    @pl.when(s == NS - 1)
    def _():
        spill_in[...] = jnp.zeros_like(spill_in)

    @pl.when(s == 0)
    def _():
        prow[...] = jnp.zeros_like(prow)

    partners = (
        12 + 3 + 3 + 1 + 1
        + jnp.where(q == x, 0, 1)
        + jnp.where(s > 0, 1, 0) + jnp.where(s < NS - 1, 1, 0)
        + jnp.where(is_att, jnp.where(att_w == r, 30, 32), 0)
    )
    pl.semaphore_wait(barrier, partners)

    @pl.when(s > 0)
    def _():
        spill_copy.start()

    wa_flow(start)
    kv_flow(send)
    wb_flow(start)

    @pl.when(s < NS - 1)
    def _():
        spill_copy.wait_recv()

    last = lax.broadcasted_iota(jnp.int32, (64, D), 0).astype(F32) == count - 1.0
    group_grad = gext[0:64] + jnp.where(last, spill_in[0:1], 0.0)
    g_hi = group_grad.astype(BF16)
    g_bf[...] = g_hi
    g_flow(send)
    landed(w_in.at[pl.ds(0, 48)], wa_recv)
    wc_flow(start)
    landed(g_bf, g_recv)
    gx_flow(start)
    g_lo = (group_grad - g_hi.astype(F32)).astype(BF16)
    byte_grad[0] = (upstream.astype(F32) + nn(picked_t, g_hi) + nn(picked_t, g_lo)).astype(BF16)

    @pl.when(is_att)
    def _():
        landed(kv.at[pl.ds(16 * r, 16)], kv_recv)
        fw_flow(start)

    landed(wq.at[0, pl.ds(0, 3), pl.ds(0, 48)], wb_recv)
    landed(wq.at[0, pl.ds(0, 3), pl.ds(0, 48)], wc_recv)
    wd_flow(start)
    landed(wq.at[:, :, pl.ds(0, 48)], wd_recv)
    landed(gq.at[pl.ds(0, 3)], gx_recv)

    g_all = gq[...].reshape(256, D)
    w_all = wq[...].reshape(D, D)
    dop[...] = nn(g_all, w_all).astype(BF16).reshape(4, 64, D)
    do_flow(send)

    @pl.when(is_att)
    def _():
        landed(kv.at[pl.ds(0, 16), pl.ds(0, 144)], fw_recv)
        kt[...] = kv[:, 0:64, :].reshape(2048, HEAD_DIM).T
        vt[...] = kv[:, 64:128, :].reshape(2048, HEAD_DIM).T
        lane = lax.broadcasted_iota(jnp.int32, (1, 128), 1).astype(F32)
        for p in range(16):
            c0 = kv[2 * p, 128:144, :].astype(F32)[0:1]
            c1 = kv[2 * p + 1, 128:144, :].astype(F32)[0:1]
            live = jnp.where(lane < 64.0, jnp.where(lane < c0, 1.0, 0.0), jnp.where(lane - 64.0 < c1, 1.0, 0.0))
            row = jnp.where(live > 0.0, lane + 128.0 * p, FAR_KEY)
            kkb[:, p * 128:(p + 1) * 128] = jnp.broadcast_to(row, (8, 128))

        def forward(i, _):
            slot = lax.broadcasted_iota(jnp.int32, (64, 128), 0).astype(F32)
            places, queries = [], []
            for mm in range(2):
                for k in range(2):
                    block = 8 * (2 * r + k) + 2 * i + mm
                    cnt = kv[block, 128:144, :].astype(F32)[0:1]
                    base = (block * 64).astype(F32)
                    places.append(jnp.where(slot < cnt, slot + base, FAR_QUERY))
                    queries.append(kv[block, 144:208, :])
            place = jnp.concatenate(places, axis=0)
            place = jnp.concatenate([place] * 16, axis=1)
            scores = nn(jnp.concatenate(queries, axis=0), kt[...])
            scores = jnp.where(jnp.broadcast_to(kkb[0:1], (256, 2048)) <= place, scores, -jnp.inf)
            top = jnp.max(scores, axis=1, keepdims=True)
            attention = jnp.exp2((scores - top) * SCALE_LOG2E)
            total = jnp.sum(attention, axis=1, keepdims=True)
            rounded = attention.astype(BF16)
            probs[i] = rounded
            inverse = 1.0 / total
            inv[i] = jnp.broadcast_to(inverse, (256, HEAD_DIM))
            out = nn(rounded, kv[:, 64:128, :].reshape(2048, HEAD_DIM)) * inverse
            a_out[pl.ds(2 * i, 2)] = out.astype(BF16).reshape(2, 2, 64, HEAD_DIM)
            a_flow(send, 2 * i)
            a_flow(send, 2 * i + 1)
            return 0

        lax.fori_loop(0, 4, forward, 0)

    @pl.when(is_att)
    def _():
        landed(dob, do_recv)
        acc[...] = jnp.zeros_like(acc)

        def backward(i, _):
            queries = jnp.concatenate(
                [kv[8 * (2 * r + k) + 2 * i + mm, 144:208, :] for mm in range(2) for k in range(2)], axis=0)
            grad = dob[0, pl.ds(2 * i, 2)].astype(F32)
            for j in range(1, 4):
                grad = grad + dob[j, pl.ds(2 * i, 2)].astype(F32)
            grad = grad.reshape(256, HEAD_DIM).astype(BF16).astype(F32)
            grad = (grad * inv[i]).astype(BF16)
            attended = a_out[pl.ds(2 * i, 2)].reshape(256, HEAD_DIM)
            dots = jnp.sum(grad.astype(F32) * attended.astype(F32), axis=1, keepdims=True)
            flow = nn(grad, vt[...])
            weights = probs[i]
            dscore = (weights.astype(F32) * (flow - dots)).astype(BF16)
            dq = nn(dscore, kv[:, 0:64, :].reshape(2048, HEAD_DIM)) * SCALE
            dqb[pl.ds(2 * i, 2)] = dq.astype(BF16).reshape(2, 2, 64, HEAD_DIM)
            dq_flow(send, 2 * i)
            dq_flow(send, 2 * i + 1)
            dk = nn(queries.T, dscore)
            dv = nn(grad.T, weights)
            for c in range(2):
                cols = slice(1024 * c, 1024 * (c + 1))
                acc[c, 0] += dk[:, cols]
                acc[c, 1] += dv[:, cols]
            return 0

        lax.fori_loop(0, 4, backward, 0)
        ex_copy.start()
        ex_copy.wait_recv()
        dkf[0] = ((acc[r, 0] + sib[0]) * SCALE).T.astype(BF16).reshape(16, 64, HEAD_DIM)
        dkf[1] = (acc[r, 1] + sib[1]).T.astype(BF16).reshape(16, 64, HEAD_DIM)

        def out(j, _):
            dkv_flow(send, j)
            return 0

        lax.fori_loop(0, 16, out, 0)

    landed(ab, a_recv)
    a_all = ab[...].reshape(256, D)
    wgp[...] = nn(gq[...].reshape(256, D).T, a_all).reshape(2, 4, 96, D)
    wgs[...] = wgp[:, :, pl.ds(pl.multiple_of(48 * (1 - r), 16), 48)].astype(BF16)
    w0_flow(start)
    pp[...] = nt(a_all, wq[...].reshape(D, D)).astype(BF16).reshape(4, 64, D)
    px_flow(start)
    landed(wg0, w0_recv)
    wh[...] = (wgp[:, :, mine48] + wg0[...].astype(F32)).astype(BF16)
    w1_flow(start)

    landed(p1.at[pl.ds(0, 3)], px_recv)
    p1[x] = pp[x]
    ps[...] = (p1[0].astype(F32) + p1[1].astype(F32) + p1[2].astype(F32) + p1[3].astype(F32)).astype(BF16)
    p_flow(send)

    landed(wg1.at[pl.ds(0, 3)], w1_recv)
    wg1[y] = wh[:, y]
    total_w = wg1[0].astype(F32)
    for i in range(1, 4):
        total_w = total_w + wg1[i].astype(F32)
    wt[...] = total_w.astype(BF16)
    w2_flow(start)

    landed(pr, p_recv)
    group_out = (grows[...] + pr[...].astype(F32)).astype(BF16)
    lrow[...] = jnp.broadcast_to(
        jnp.sum(jnp.where(last, group_out.astype(F32), 0.0), axis=0, keepdims=True), (16, D)
    ).astype(BF16)

    @pl.when(s < NS - 1)
    def _():
        row_copy.start()

    landed(wg2, w2_recv)
    wsum[...] = wt[zp].astype(F32) + wg2[...].astype(F32)
    ws_flow(start)
    wg_out[mine48] = wsum[...]

    @pl.when(s > 0)
    def _():
        row_copy.wait_recv()

    rows = jnp.concatenate([group_out, prow[...]], axis=0)
    cross = nt(rows, up[0])
    part = jnp.sum(sel_s[...] * cross, axis=0, keepdims=True)
    cpart[...] = jnp.broadcast_to(part, (8, NB))
    call[x] = cpart[...]
    c_flow(start)
    landed(call.at[pl.ds(0, 3)], c_recv)
    conf_grad[...] = (call[0] + call[1] + call[2] + call[3])[0:1]

    landed(wsum, ws_recv)
    kv_flow(sent)
    g_flow(sent)
    do_flow(sent)
    p_flow(sent)
    for flow in (wa_flow, wb_flow, wc_flow, wd_flow, gx_flow, px_flow, w0_flow, w1_flow, w2_flow, ws_flow, c_flow):
        flow(finish)

    @pl.when(s > 0)
    def _():
        spill_copy.wait_send()

    @pl.when(s < NS - 1)
    def _():
        row_copy.wait_send()

    @pl.when(is_att)
    def _():
        fw_flow(finish)
        ex_copy.wait_send()

        def one(j, _):
            a_flow(sent, j)
            dq_flow(sent, j)
            return 0

        lax.fori_loop(0, 8, one, 0)

        def two(j, _):
            dkv_flow(sent, j)
            return 0

        lax.fori_loop(0, 16, two, 0)

    landed(dq_out, dq_recv)
    landed(dk_out, dk_recv)
    landed(dv_out, dv_recv)


def local(byte_states, boundary, confidence, query_rows, key_rows, value_rows, out_weight, upstream):
    vmem = pl.BlockSpec(memory_space=pltpu.VMEM)
    dma = pltpu.SemaphoreType.DMA
    rows = jax.ShapeDtypeStruct((1, CAP, D), BF16)
    return pl.pallas_call(
        kernel,
        out_shape=(
            jax.ShapeDtypeStruct((1, NB, D), BF16),
            jax.ShapeDtypeStruct((1, NB), F32),
            rows, rows, rows,
            jax.ShapeDtypeStruct((96, D), F32),
        ),
        in_specs=[vmem] * 8,
        out_specs=(vmem,) * 6,
        scratch_shapes=[
            pltpu.VMEM((NH, 208, 128), BF16),
            pltpu.VMEM((NS, 208, 128), BF16),
            pltpu.VMEM((2, 4, 96, D), BF16),
            pltpu.VMEM((80, D), F32),
            pltpu.VMEM((8, D), F32),
            pltpu.VMEM((64, D), BF16),
            pltpu.VMEM((4, 64, D), BF16),
            pltpu.VMEM((4, 64, D), BF16),
            pltpu.VMEM((4, 8, 2, 64, 128), BF16),
            pltpu.VMEM((128, 2048), BF16),
            pltpu.VMEM((128, 2048), BF16),
            pltpu.VMEM((8, 2048), F32),
            pltpu.VMEM((4, 256, 2048), BF16),
            pltpu.VMEM((4, 256, 128), F32),
            pltpu.VMEM((8, 2, 64, 128), BF16),
            pltpu.VMEM((4, 64, D), BF16),
            pltpu.VMEM((4, 64, D), BF16),
            pltpu.VMEM((4, 64, D), BF16),
            pltpu.VMEM((64, D), BF16),
            pltpu.VMEM((64, D), BF16),
            pltpu.VMEM((2, 4, 96, D), F32),
            pltpu.VMEM((2, 4, 48, D), BF16),
            pltpu.VMEM((2, 4, 48, D), BF16),
            pltpu.VMEM((2, 4, 48, D), BF16),
            pltpu.VMEM((4, 2, 48, D), BF16),
            pltpu.VMEM((2, 48, D), BF16),
            pltpu.VMEM((48, D), BF16),
            pltpu.VMEM((48, D), F32),
            pltpu.VMEM((16, D), BF16),
            pltpu.VMEM((16, D), BF16),
            pltpu.VMEM((8, NB), F32),
            pltpu.VMEM((4, 8, NB), F32),
            pltpu.VMEM((8, 2, 64, 128), BF16),
            pltpu.VMEM((2, 2, 128, 1024), F32),
            pltpu.VMEM((2, 128, 1024), F32),
            pltpu.VMEM((2, 16, 64, 128), BF16),
            pltpu.VMEM((80, NB), F32),
            pltpu.VMEM((64, D), F32),
            dma((6,)), dma,
            dma, dma,
            dma, dma,
            dma((3,)), dma,
            dma((3,)), dma,
            dma, dma,
            dma, dma,
            dma, dma,
            dma((3,)), dma,
            dma((12,)), dma,
            dma((32,)), dma,
            dma((3,)), dma,
            dma, dma,
            dma, dma,
            dma((3,)), dma,
            dma, dma,
            dma, dma,
            dma, dma,
            dma((3,)), dma,
            dma((16,)), dma,
            dma((16,)), dma,
            dma((16,)), dma,
            dma, dma,
        ],
        compiler_params=pltpu.CompilerParams(
            collective_id=0, has_side_effects=True, vmem_limit_bytes=56 * 1024 * 1024
        ),
        cost_estimate=pl.CostEstimate(flops=8_000_000_000, bytes_accessed=20_000_000, transcendentals=3_000_000),
    )(byte_states, boundary, confidence, query_rows, key_rows, value_rows, out_weight, upstream)


def solution(mesh):
    split = P("rep", "seq", "head")
    bytes_ = P("rep", "seq")
    return jax.shard_map(
        local,
        mesh=mesh,
        in_specs=(split, bytes_, bytes_, split, split, split, P("seq", "head"), split),
        out_specs=(split, bytes_, split, split, split, P("seq", "head")),
        check_vma=False,
    )
```

```python
import jax
import jax.numpy as jnp
from jax import lax
from jax.experimental import pallas as pl
from jax.experimental.pallas import tpu as pltpu
from jax.sharding import PartitionSpec as P

MESH = pl.DeviceIdType.MESH
F32, BF16 = jnp.float32, jnp.bfloat16

HEAD_DIM = 128
NS = 32
NH = 6
D = 768
CAP = 64
NB = 256
SCALE = HEAD_DIM ** -0.5
SCALE_LOG2E = SCALE * 1.4426950408889634
FAR_QUERY = 4096.0
FAR_KEY = 8192.0


def att_seq(h, w):
    return lax.div((2 * h + w) * 8, 3)


def nt(a, b):
    return lax.dot_general(a, b, (((1,), (1,)), ((), ())), preferred_element_type=F32)


def nn(a, b):
    return jnp.dot(a, b, preferred_element_type=F32)


def kernel(
    states, starts, conf, q_in, k_in, v_in, w_in, up,
    byte_grad, conf_grad, dq_out, dk_out, dv_out, wg_out,
    stage, kv, wq, gext, spill_in, g_bf, gq, dop, dob,
    kt, vt, kkb, probs, inv, a_out, ab, pp, p1, ps, pr, wgp, wgs, wg0, wh, wg1, wt, wg2, wsum,
    lrow, prow, cpart, call, dqb, acc, sib, dkf, sel_s, grows,
    kv_send, kv_recv, fw_send, fw_recv, wa_send, wa_recv, wb_send, wb_recv, wc_send, wc_recv, wd_send, wd_recv,
    sp_send, sp_recv, g_send, g_recv, gx_send, gx_recv,
    do_send, do_recv, a_send, a_recv, px_send, px_recv, p_send, p_recv,
    w0_send, w0_recv, w1_send, w1_recv, w2_send, w2_recv, ws_send, ws_recv,
    lr_send, lr_recv, c_send, c_recv, dq_send, dq_recv, dk_send, dk_recv, dv_send, dv_recv,
    ex_send, ex_recv,
):
    s = lax.axis_index("seq")
    x = lax.axis_index("head")
    r = lax.axis_index("rep")
    q = lax.div(s, 8)
    m = lax.rem(s, 8)
    zp = lax.div(m, 4)
    y = lax.rem(m, 4)
    half = lax.div(q, 2)
    att = lax.div(3 * s + 7, 8)
    is_att = jnp.logical_and(lax.div(att * 8, 3) == s, att < 12)
    att_h = lax.div(att, 2)
    att_w = lax.rem(att, 2)

    def same(t):
        return jnp.logical_and(jnp.logical_and(t[0] == s, t[1] == x), t[2] == r)

    def send(src, dst, ssem, rsem, t):
        mine = same(t)

        @pl.when(jnp.logical_not(mine))
        def _():
            pltpu.make_async_remote_copy(src, dst, ssem, rsem, device_id=t, device_id_type=MESH).start()

        @pl.when(mine)
        def _():
            pltpu.make_async_copy(src, dst, rsem).start()

    def sent(src, dst, ssem, rsem, t):
        @pl.when(jnp.logical_not(same(t)))
        def _():
            pltpu.make_async_remote_copy(src, dst, ssem, rsem, device_id=t, device_id_type=MESH).wait_send()

    def landed(ref, rsem):
        pltpu.make_async_copy(ref, ref, rsem).wait()

    def remote(src, dst, ssem, rsem, t):
        return pltpu.make_async_remote_copy(src, dst, ssem, rsem, device_id=t, device_id_type=MESH)

    def start(*a):
        remote(*a).start()

    def finish(*a):
        remote(*a).wait_send()

    def lanes(h):
        return pl.ds(h * HEAD_DIM if isinstance(h, int) else pl.multiple_of(h * HEAD_DIM, HEAD_DIM), HEAD_DIM)

    mine48 = pl.ds(pl.multiple_of(48 * r, 16), 48)
    z_peer = (s + 4 - 8 * zp, x, r)
    sib_id = (s, x, 1 - r)

    def y_peer(i):
        return (s - y + lax.rem(y + i, 4), x, r)

    def x_peer(i):
        return (s, lax.rem(x + i, 4), r)

    def kv_flow(op):
        for h in range(NH):
            op(stage.at[h], kv.at[s], kv_send.at[h], kv_recv, (att_seq(h, r), x, half))

    def wa_flow(op):
        op(w_in.at[mine48], wq.at[zp, y, mine48], wa_send, wa_recv, z_peer)

    def wb_flow(op):
        for i in range(1, 4):
            op(w_in.at[mine48], wq.at[zp, y, mine48], wb_send.at[i - 1], wb_recv, y_peer(i))

    def wc_flow(op):
        for i in range(1, 4):
            op(wq.at[1 - zp, y, mine48], wq.at[1 - zp, y, mine48], wc_send.at[i - 1], wc_recv, y_peer(i))

    def wd_flow(op):
        op(wq.at[:, :, mine48], wq.at[:, :, mine48], wd_send, wd_recv, sib_id)

    turned = (8 * x + m, q, r)

    def g_flow(op):
        op(g_bf, gq.at[q], g_send, g_recv, turned)

    def gx_flow(op):
        for i in range(1, 4):
            op(gq.at[x], gq.at[x], gx_send.at[i - 1], gx_recv, x_peer(i))

    def do_flow(op):
        for h in range(NH):
            for c in range(2):
                op(dop.at[pl.ds(2 * c, 2), :, lanes(h)], dob.at[q, m], do_send.at[2 * h + c], do_recv,
                   (att_seq(h, r), x, c))

    def a_flow(op, mm):
        for i in range(4):
            op(a_out.at[mm], ab.at[pl.ds(2 * r, 2), :, lanes(att_h)], a_send.at[mm * 4 + i], a_recv,
               (8 * i + mm, x, att_w))

    def px_flow(op):
        for i in range(1, 4):
            op(pp.at[lax.rem(x + i, 4)], p1.at[x], px_send.at[i - 1], px_recv, x_peer(i))

    def p_flow(op):
        op(ps, pr, p_send, p_recv, turned)

    def w0_flow(op):
        op(wgs, wg0, w0_send, w0_recv, sib_id)

    def w1_flow(op):
        for i in range(1, 4):
            op(wh.at[:, lax.rem(y + i, 4)], wg1.at[y], w1_send.at[i - 1], w1_recv, y_peer(i))

    def w2_flow(op):
        op(wt.at[1 - zp], wg2, w2_send, w2_recv, z_peer)

    def ws_flow(op):
        op(wsum, wg_out.at[mine48], ws_send, ws_recv, sib_id)

    def c_flow(op):
        for i in range(1, 4):
            op(cpart, call.at[x], c_send.at[i - 1], c_recv, x_peer(i))

    def dq_flow(op, mm):
        for k in range(2):
            op(dqb.at[mm, k], dq_out.at[0, :, lanes(att_h)], dq_send.at[mm * 2 + k], dq_recv,
               (8 * (2 * r + k) + mm, x, att_w))

    def dkv_flow(op, j):
        op(dkf.at[0, j], dk_out.at[0, :, lanes(att_h)], dk_send.at[j], dk_recv, (16 * r + j, x, att_w))
        op(dkf.at[1, j], dv_out.at[0, :, lanes(att_h)], dv_send.at[j], dv_recv, (16 * r + j, x, att_w))

    def fw_flow(op):
        part = kv.at[pl.ds(16 * r, 16), pl.ds(0, 144)]
        op(part, part, fw_send, fw_recv, sib_id)

    spill_copy = remote(gext.at[pl.ds(64, 8)], spill_in, sp_send, sp_recv, (s - 1, x, r))
    row_copy = remote(lrow, prow, lr_send, lr_recv, (s + 1, x, r))
    ex_copy = remote(acc.at[1 - r], sib, ex_send, ex_recv, sib_id)

    barrier = pltpu.get_barrier_semaphore()

    def greet(t):
        @pl.when(jnp.logical_not(same(t)))
        def _():
            pl.semaphore_signal(barrier, inc=1, device_id=t, device_id_type=MESH)

    for h in range(NH):
        for c in range(2):
            greet((att_seq(h, r), x, c))
    for i in range(1, 4):
        greet(y_peer(i))
        greet(x_peer(i))
    greet(z_peer)
    greet(turned)
    greet(sib_id)

    @pl.when(s > 0)
    def _():
        greet((s - 1, x, r))

    @pl.when(s < NS - 1)
    def _():
        greet((s + 1, x, r))

    @pl.when(is_att)
    def _():
        def one(j, _):
            greet((j, x, att_w))
            return 0

        lax.fori_loop(0, NS, one, 0)

    start_row = starts[...].astype(F32)
    before = lax.broadcasted_iota(jnp.int32, (NB, NB), 0) <= lax.broadcasted_iota(jnp.int32, (NB, NB), 1)
    tri = jnp.where(before, 1.0, 0.0).astype(BF16)
    rank = nn(jnp.broadcast_to(start_row, (16, NB)).astype(BF16), tri)[0:1] - 1.0
    count = jnp.sum(start_row, axis=1, keepdims=True)
    slot80 = lax.broadcasted_iota(jnp.int32, (80, NB), 0).astype(F32)
    want = jnp.where(slot80 < 64.0, slot80, jnp.where(slot80 == 64.0, -1.0, -2.0))
    sel = jnp.where(jnp.broadcast_to(rank, (80, NB)) == want, 1.0, 0.0)
    sel_s[...] = sel
    weight = sel * conf[...]
    w_hi = weight.astype(BF16)
    w_lo = (weight - w_hi.astype(F32)).astype(BF16)
    upstream = up[0]
    gext[...] = nn(w_hi, upstream) + nn(w_lo, upstream)
    for h in range(NH):
        cols = slice(h * HEAD_DIM, (h + 1) * HEAD_DIM)
        stage[h, 0:64] = k_in[0, :, cols]
        stage[h, 64:128] = v_in[0, :, cols]
        stage[h, 128:144] = jnp.broadcast_to(count, (16, HEAD_DIM)).astype(BF16)
        stage[h, 144:208] = q_in[0, :, cols]
    picked = sel[0:64] * start_row
    picked_t = picked.T.astype(BF16)
    grows[...] = nn(picked.astype(BF16), states[0])
    wq[zp, y, mine48] = w_in[mine48]

    @pl.when(s == NS - 1)
    def _():
        spill_in[...] = jnp.zeros_like(spill_in)

    @pl.when(s == 0)
    def _():
        prow[...] = jnp.zeros_like(prow)

    partners = (
        12 + 3 + 3 + 1 + 1
        + jnp.where(q == x, 0, 1)
        + jnp.where(s > 0, 1, 0) + jnp.where(s < NS - 1, 1, 0)
        + jnp.where(is_att, jnp.where(att_w == r, 30, 32), 0)
    )
    pl.semaphore_wait(barrier, partners)

    @pl.when(s > 0)
    def _():
        spill_copy.start()

    wa_flow(start)
    wb_flow(start)

    @pl.when(s < NS - 1)
    def _():
        spill_copy.wait_recv()

    last = lax.broadcasted_iota(jnp.int32, (64, D), 0).astype(F32) == count - 1.0
    group_grad = gext[0:64] + jnp.where(last, spill_in[0:1], 0.0)
    g_hi = group_grad.astype(BF16)
    g_bf[...] = g_hi
    g_flow(send)
    kv_flow(send)
    landed(w_in.at[pl.ds(0, 48)], wa_recv)
    wc_flow(start)
    landed(g_bf, g_recv)
    gx_flow(start)
    g_lo = (group_grad - g_hi.astype(F32)).astype(BF16)
    byte_grad[0] = (upstream.astype(F32) + nn(picked_t, g_hi) + nn(picked_t, g_lo)).astype(BF16)

    landed(wq.at[0, pl.ds(0, 3), pl.ds(0, 48)], wb_recv)
    landed(wq.at[0, pl.ds(0, 3), pl.ds(0, 48)], wc_recv)
    wd_flow(start)
    landed(wq.at[:, :, pl.ds(0, 48)], wd_recv)
    landed(gq.at[pl.ds(0, 3)], gx_recv)

    g_all = gq[...].reshape(256, D)
    w_all = wq[...].reshape(D, D)
    dop[...] = nn(g_all, w_all).astype(BF16).reshape(4, 64, D)
    do_flow(send)

    @pl.when(is_att)
    def _():
        landed(kv.at[pl.ds(16 * r, 16)], kv_recv)
        fw_flow(start)
        landed(kv.at[pl.ds(0, 16), pl.ds(0, 144)], fw_recv)
        kt[...] = kv[:, 0:64, :].reshape(2048, HEAD_DIM).T
        vt[...] = kv[:, 64:128, :].reshape(2048, HEAD_DIM).T
        lane = lax.broadcasted_iota(jnp.int32, (1, 128), 1).astype(F32)
        for p in range(16):
            c0 = kv[2 * p, 128:144, :].astype(F32)[0:1]
            c1 = kv[2 * p + 1, 128:144, :].astype(F32)[0:1]
            live = jnp.where(lane < 64.0, jnp.where(lane < c0, 1.0, 0.0), jnp.where(lane - 64.0 < c1, 1.0, 0.0))
            row = jnp.where(live > 0.0, lane + 128.0 * p, FAR_KEY)
            kkb[:, p * 128:(p + 1) * 128] = jnp.broadcast_to(row, (8, 128))

        def forward(i, _):
            slot = lax.broadcasted_iota(jnp.int32, (64, 128), 0).astype(F32)
            places, queries = [], []
            for mm in range(2):
                for k in range(2):
                    block = 8 * (2 * r + k) + 2 * i + mm
                    cnt = kv[block, 128:144, :].astype(F32)[0:1]
                    base = (block * 64).astype(F32)
                    places.append(jnp.where(slot < cnt, slot + base, FAR_QUERY))
                    queries.append(kv[block, 144:208, :])
            place = jnp.concatenate(places, axis=0)
            place = jnp.concatenate([place] * 16, axis=1)
            scores = nn(jnp.concatenate(queries, axis=0), kt[...])
            scores = jnp.where(jnp.broadcast_to(kkb[0:1], (256, 2048)) <= place, scores, -jnp.inf)
            top = jnp.max(scores, axis=1, keepdims=True)
            attention = jnp.exp2((scores - top) * SCALE_LOG2E)
            total = jnp.sum(attention, axis=1, keepdims=True)
            rounded = attention.astype(BF16)
            probs[i] = rounded
            inverse = 1.0 / total
            inv[i] = jnp.broadcast_to(inverse, (256, HEAD_DIM))
            out = nn(rounded, kv[:, 64:128, :].reshape(2048, HEAD_DIM)) * inverse
            a_out[pl.ds(2 * i, 2)] = out.astype(BF16).reshape(2, 2, 64, HEAD_DIM)
            a_flow(send, 2 * i)
            a_flow(send, 2 * i + 1)
            return 0

        lax.fori_loop(0, 4, forward, 0)

    @pl.when(is_att)
    def _():
        landed(dob, do_recv)
        acc[...] = jnp.zeros_like(acc)

        def backward(i, _):
            queries = jnp.concatenate(
                [kv[8 * (2 * r + k) + 2 * i + mm, 144:208, :] for mm in range(2) for k in range(2)], axis=0)
            grad = dob[0, pl.ds(2 * i, 2)].astype(F32)
            for j in range(1, 4):
                grad = grad + dob[j, pl.ds(2 * i, 2)].astype(F32)
            grad = grad.reshape(256, HEAD_DIM).astype(BF16).astype(F32)
            grad = (grad * inv[i]).astype(BF16)
            attended = a_out[pl.ds(2 * i, 2)].reshape(256, HEAD_DIM)
            dots = jnp.sum(grad.astype(F32) * attended.astype(F32), axis=1, keepdims=True)
            flow = nn(grad, vt[...])
            weights = probs[i]
            dscore = (weights.astype(F32) * (flow - dots)).astype(BF16)
            dq = nn(dscore, kv[:, 0:64, :].reshape(2048, HEAD_DIM)) * SCALE
            dqb[pl.ds(2 * i, 2)] = dq.astype(BF16).reshape(2, 2, 64, HEAD_DIM)
            dq_flow(send, 2 * i)
            dq_flow(send, 2 * i + 1)
            dk = nn(queries.T, dscore)
            dv = nn(grad.T, weights)
            for c in range(2):
                cols = slice(1024 * c, 1024 * (c + 1))
                acc[c, 0] += dk[:, cols]
                acc[c, 1] += dv[:, cols]
            return 0

        lax.fori_loop(0, 4, backward, 0)
        ex_copy.start()
    landed(ab, a_recv)
    a_all = ab[...].reshape(256, D)
    wgp[...] = nn(gq[...].reshape(256, D).T, a_all).reshape(2, 4, 96, D)
    wgs[...] = wgp[:, :, pl.ds(pl.multiple_of(48 * (1 - r), 16), 48)].astype(BF16)
    w0_flow(start)
    pp[...] = nt(a_all, wq[...].reshape(D, D)).astype(BF16).reshape(4, 64, D)
    px_flow(start)

    @pl.when(is_att)
    def _():
        ex_copy.wait_recv()
        dkf[0] = ((acc[r, 0] + sib[0]) * SCALE).T.astype(BF16).reshape(16, 64, HEAD_DIM)
        dkf[1] = (acc[r, 1] + sib[1]).T.astype(BF16).reshape(16, 64, HEAD_DIM)

        def out(j, _):
            dkv_flow(send, j)
            return 0

        lax.fori_loop(0, 16, out, 0)

    landed(wg0, w0_recv)
    wh[...] = (wgp[:, :, mine48] + wg0[...].astype(F32)).astype(BF16)
    w1_flow(start)

    landed(p1.at[pl.ds(0, 3)], px_recv)
    p1[x] = pp[x]
    ps[...] = (p1[0].astype(F32) + p1[1].astype(F32) + p1[2].astype(F32) + p1[3].astype(F32)).astype(BF16)
    p_flow(send)

    landed(wg1.at[pl.ds(0, 3)], w1_recv)
    wg1[y] = wh[:, y]
    total_w = wg1[0].astype(F32)
    for i in range(1, 4):
        total_w = total_w + wg1[i].astype(F32)
    wt[...] = total_w.astype(BF16)
    w2_flow(start)

    landed(pr, p_recv)
    group_out = (grows[...] + pr[...].astype(F32)).astype(BF16)
    lrow[...] = jnp.broadcast_to(
        jnp.sum(jnp.where(last, group_out.astype(F32), 0.0), axis=0, keepdims=True), (16, D)
    ).astype(BF16)

    @pl.when(s < NS - 1)
    def _():
        row_copy.start()

    landed(wg2, w2_recv)
    wsum[...] = wt[zp].astype(F32) + wg2[...].astype(F32)
    ws_flow(start)
    wg_out[mine48] = wsum[...]

    @pl.when(s > 0)
    def _():
        row_copy.wait_recv()

    rows = jnp.concatenate([group_out, prow[...]], axis=0)
    cross = nt(rows, up[0])
    part = jnp.sum(sel_s[...] * cross, axis=0, keepdims=True)
    cpart[...] = jnp.broadcast_to(part, (8, NB))
    call[x] = cpart[...]
    c_flow(start)
    landed(call.at[pl.ds(0, 3)], c_recv)
    conf_grad[...] = (call[0] + call[1] + call[2] + call[3])[0:1]

    landed(wsum, ws_recv)
    kv_flow(sent)
    g_flow(sent)
    do_flow(sent)
    p_flow(sent)
    for flow in (wa_flow, wb_flow, wc_flow, wd_flow, gx_flow, px_flow, w0_flow, w1_flow, w2_flow, ws_flow, c_flow):
        flow(finish)

    @pl.when(s > 0)
    def _():
        spill_copy.wait_send()

    @pl.when(s < NS - 1)
    def _():
        row_copy.wait_send()

    @pl.when(is_att)
    def _():
        fw_flow(finish)
        ex_copy.wait_send()

        def one(j, _):
            a_flow(sent, j)
            dq_flow(sent, j)
            return 0

        lax.fori_loop(0, 8, one, 0)

        def two(j, _):
            dkv_flow(sent, j)
            return 0

        lax.fori_loop(0, 16, two, 0)

    landed(dq_out, dq_recv)
    landed(dk_out, dk_recv)
    landed(dv_out, dv_recv)


def hand_over(*refs):
    held, sems = refs[12:18], refs[18]
    come = [pltpu.make_async_copy(refs[i], held[i], sems.at[i]) for i in range(6)]
    leave = [pltpu.make_async_copy(held[i], refs[6 + i], sems.at[6 + i]) for i in range(6)]
    for copy in come:
        copy.start()
    for i in range(6):
        come[i].wait()
        leave[i].start()
    for copy in leave:
        copy.wait()


def local(byte_states, boundary, confidence, query_rows, key_rows, value_rows, out_weight, upstream):
    vmem = pl.BlockSpec(memory_space=pltpu.VMEM)
    dma = pltpu.SemaphoreType.DMA
    rows = jax.ShapeDtypeStruct((1, CAP, D), BF16)
    shapes = (
        jax.ShapeDtypeStruct((1, NB, D), BF16),
        jax.ShapeDtypeStruct((1, NB), F32),
        rows, rows, rows,
        jax.ShapeDtypeStruct((96, D), F32),
    )
    parts = pl.pallas_call(
        kernel,
        out_shape=shapes,
        in_specs=[vmem] * 8,
        out_specs=(vmem,) * 6,
        scratch_shapes=[
            pltpu.VMEM((NH, 208, 128), BF16),
            pltpu.VMEM((NS, 208, 128), BF16),
            pltpu.VMEM((2, 4, 96, D), BF16),
            pltpu.VMEM((80, D), F32),
            pltpu.VMEM((8, D), F32),
            pltpu.VMEM((64, D), BF16),
            pltpu.VMEM((4, 64, D), BF16),
            pltpu.VMEM((4, 64, D), BF16),
            pltpu.VMEM((4, 8, 2, 64, 128), BF16),
            pltpu.VMEM((128, 2048), BF16),
            pltpu.VMEM((128, 2048), BF16),
            pltpu.VMEM((8, 2048), F32),
            pltpu.VMEM((4, 256, 2048), BF16),
            pltpu.VMEM((4, 256, 128), F32),
            pltpu.VMEM((8, 2, 64, 128), BF16),
            pltpu.VMEM((4, 64, D), BF16),
            pltpu.VMEM((4, 64, D), BF16),
            pltpu.VMEM((4, 64, D), BF16),
            pltpu.VMEM((64, D), BF16),
            pltpu.VMEM((64, D), BF16),
            pltpu.VMEM((2, 4, 96, D), F32),
            pltpu.VMEM((2, 4, 48, D), BF16),
            pltpu.VMEM((2, 4, 48, D), BF16),
            pltpu.VMEM((2, 4, 48, D), BF16),
            pltpu.VMEM((4, 2, 48, D), BF16),
            pltpu.VMEM((2, 48, D), BF16),
            pltpu.VMEM((48, D), BF16),
            pltpu.VMEM((48, D), F32),
            pltpu.VMEM((16, D), BF16),
            pltpu.VMEM((16, D), BF16),
            pltpu.VMEM((8, NB), F32),
            pltpu.VMEM((4, 8, NB), F32),
            pltpu.VMEM((8, 2, 64, 128), BF16),
            pltpu.VMEM((2, 2, 128, 1024), F32),
            pltpu.VMEM((2, 128, 1024), F32),
            pltpu.VMEM((2, 16, 64, 128), BF16),
            pltpu.VMEM((80, NB), F32),
            pltpu.VMEM((64, D), F32),
            dma((6,)), dma,
            dma, dma,
            dma, dma,
            dma((3,)), dma,
            dma((3,)), dma,
            dma, dma,
            dma, dma,
            dma, dma,
            dma((3,)), dma,
            dma((12,)), dma,
            dma((32,)), dma,
            dma((3,)), dma,
            dma, dma,
            dma, dma,
            dma((3,)), dma,
            dma, dma,
            dma, dma,
            dma, dma,
            dma((3,)), dma,
            dma((16,)), dma,
            dma((16,)), dma,
            dma((16,)), dma,
            dma, dma,
        ],
        compiler_params=pltpu.CompilerParams(
            collective_id=0, has_side_effects=True, vmem_limit_bytes=56 * 1024 * 1024
        ),
        cost_estimate=pl.CostEstimate(flops=8_000_000_000, bytes_accessed=20_000_000, transcendentals=3_000_000),
    )(byte_states, boundary, confidence, query_rows, key_rows, value_rows, out_weight, upstream)
    whole = pl.BlockSpec(memory_space=pl.ANY)
    return pl.pallas_call(
        hand_over,
        out_shape=shapes,
        in_specs=[whole] * 6,
        out_specs=(whole,) * 6,
        scratch_shapes=[pltpu.VMEM(shape.shape, shape.dtype) for shape in shapes] + [dma((12,))],
        compiler_params=pltpu.CompilerParams(vmem_limit_bytes=60 * 1024 * 1024),
    )(*parts)


def solution(mesh):
    split = P("rep", "seq", "head")
    bytes_ = P("rep", "seq")
    return jax.shard_map(
        local,
        mesh=mesh,
        in_specs=(split, bytes_, bytes_, split, split, split, P("seq", "head"), split),
        out_specs=(split, bytes_, split, split, split, P("seq", "head")),
        check_vma=False,
    )
```

```python
import jax
import jax.numpy as jnp
from jax import lax
from jax.experimental import pallas as pl
from jax.experimental.pallas import tpu as pltpu
from jax.sharding import PartitionSpec as P

MESH = pl.DeviceIdType.MESH
F32, BF16 = jnp.float32, jnp.bfloat16

HEAD_DIM = 128
NS = 32
NH = 6
D = 768
CAP = 64
NB = 256
SCALE = HEAD_DIM ** -0.5
SCALE_LOG2E = SCALE * 1.4426950408889634
FAR_QUERY = 4096.0
FAR_KEY = 8192.0


def att_seq(h, w):
    return lax.div((2 * h + w) * 8, 3)


def nt(a, b):
    return lax.dot_general(a, b, (((1,), (1,)), ((), ())), preferred_element_type=F32)


def nn(a, b):
    return jnp.dot(a, b, preferred_element_type=F32)


def kernel(
    states, starts, conf, q_in, k_in, v_in, w_in, up,
    byte_grad, conf_grad, dq_out, dk_out, dv_out, wg_out,
    stage, kv, wq, gext, spill_in, perm, pack, gp, gr, gq, dop, dr, og, dob,
    kt, vt, kkb, probs, inv, a_out, ab, pp, p1, ps4, pr, wgp, wgs, wg0, wh, wg1, rl, rs, wsum,
    lrow, prow, cpart, call, dqb, acc, sib, dkf, sel_s, grows,
    kv_send, kv_recv, fw_send, fw_recv, wa_send, wa_recv, wb_send, wb_recv, wd_send, wd_recv,
    sp_send, sp_recv, g_send, g_recv, gx_send, gx_recv, dr_send, dr_recv,
    do_send, do_recv, a_send, a_recv, ay_send, ay_recv, px_send, px_recv, p_send, p_recv,
    w0_send, w0_recv, w1_send, w1_recv, rl_send, rl_recv, ws_send, ws_recv,
    lr_send, lr_recv, c_send, c_recv, dq_send, dq_recv, dk_send, dk_recv, dv_send, dv_recv,
    ex_send, ex_recv,
):
    s = lax.axis_index("seq")
    x = lax.axis_index("head")
    r = lax.axis_index("rep")
    q = lax.div(s, 8)
    m = lax.rem(s, 8)
    z = lax.div(s, 4)
    y = lax.rem(m, 4)
    half = lax.div(q, 2)
    att = lax.div(3 * s + 7, 8)
    is_att = jnp.logical_and(lax.div(att * 8, 3) == s, att < 12)
    att_h = lax.div(att, 2)
    att_w = lax.rem(att, 2)

    def same(t):
        return jnp.logical_and(jnp.logical_and(t[0] == s, t[1] == x), t[2] == r)

    def send(src, dst, ssem, rsem, t):
        mine = same(t)

        @pl.when(jnp.logical_not(mine))
        def _():
            pltpu.make_async_remote_copy(src, dst, ssem, rsem, device_id=t, device_id_type=MESH).start()

        @pl.when(mine)
        def _():
            pltpu.make_async_copy(src, dst, rsem).start()

    def sent(src, dst, ssem, rsem, t):
        @pl.when(jnp.logical_not(same(t)))
        def _():
            pltpu.make_async_remote_copy(src, dst, ssem, rsem, device_id=t, device_id_type=MESH).wait_send()

    def landed(ref, rsem):
        pltpu.make_async_copy(ref, ref, rsem).wait()

    def remote(src, dst, ssem, rsem, t):
        return pltpu.make_async_remote_copy(src, dst, ssem, rsem, device_id=t, device_id_type=MESH)

    def start(*a):
        remote(*a).start()

    def finish(*a):
        remote(*a).wait_send()

    def lanes(h):
        return pl.ds(h * HEAD_DIM if isinstance(h, int) else pl.multiple_of(h * HEAD_DIM, HEAD_DIM), HEAD_DIM)

    mine48 = pl.ds(pl.multiple_of(48 * r, 16), 48)
    sib_id = (s, x, 1 - r)

    def y_peer(i):
        return (s - y + lax.rem(y + i, 4), x, r)

    def z_place(i):
        return lax.rem(z + i, 8)

    def z_peer(i):
        return (4 * z_place(i) + y, x, r)

    def x_peer(i):
        return (s, lax.rem(x + i, 4), r)

    def kv_flow(op):
        for i in range(NH):
            h = lax.rem(s + 3 * r + i, NH)
            op(stage.at[h], kv.at[s], kv_send.at[i], kv_recv, (att_seq(h, r), x, half))

    even = lax.rem(z, 2) == 0

    def wa_flow(op):
        for j, i in enumerate((1, 7, 2, 6)):
            op(w_in.at[mine48], wq.at[z, mine48], wa_send.at[j], wa_recv.at[j], z_peer(i))

    def wb_flow(op):
        for j, (block, i) in enumerate(((6, 1), (2, 7), (jnp.where(even, 6, 2), jnp.where(even, 2, 6)))):
            part = wq.at[z_place(block), mine48]
            op(part, part, wb_send.at[j], wb_recv, z_peer(i))

    def wd_flow(op):
        op(wq.at[:, mine48], wq.at[:, mine48], wd_send, wd_recv, sib_id)

    def g_flow(op):
        for i in range(4):
            op(gp.at[i], gr.at[x], g_send.at[i], g_recv, (4 * z + i, y, r))

    def gx_flow(op):
        for i in range(1, 4):
            op(gq.at[x], gq.at[x], gx_send.at[i - 1], gx_recv, x_peer(i))

    def dr_flow(op):
        for i in range(1, 4):
            op(dop.at[lax.rem(y + i, 4)], dr.at[y], dr_send.at[i - 1], dr_recv, y_peer(i))

    def do_flow(op):
        for i in range(NH):
            h = lax.rem(s + 3 * r + i, NH)
            op(og.at[:, lanes(h)], dob.at[m, lax.rem(q, 2)], do_send.at[i], do_recv, (att_seq(h, r), x, half))

    def a_flow(op, mm):
        for k in range(2):
            op(a_out.at[mm, k], ab.at[lax.rem(mm, 4), :, lanes(att_h)], a_send.at[mm * 2 + k], a_recv,
               (8 * (2 * r + k) + mm, x, att_w))

    def ay_flow(op):
        for i in range(1, 4):
            op(ab.at[y], ab.at[y], ay_send.at[i - 1], ay_recv, y_peer(i))

    def px_flow(op):
        for i in range(1, 4):
            op(pp.at[lax.rem(x + i, 4)], p1.at[x], px_send.at[i - 1], px_recv, x_peer(i))

    def p_flow(op):
        for i in range(4):
            op(ps4.at[i], pr.at[y], p_send.at[i], p_recv, (4 * z + x, i, r))

    def w0_flow(op):
        op(wgs, wg0, w0_send, w0_recv, sib_id)

    def w1_flow(op):
        for j, i in enumerate((1, 7)):
            op(wh.at[z_place(i)], wg1.at[j], w1_send.at[j], w1_recv.at[j], z_peer(i))
        for j, (block, i) in enumerate(((3, 1), (5, 7), (4, jnp.where(even, 2, 6)))):
            op(wh.at[z_place(block)], rl.at[j], rl_send.at[j], rl_recv.at[j], z_peer(i))

    def w2_flow(op):
        for j, i in enumerate((2, 6)):
            op(rs.at[j], wg1.at[2 + j], w1_send.at[2 + j], w1_recv.at[2 + j], z_peer(i))

    def ws_flow(op):
        op(wsum, wg_out.at[mine48], ws_send, ws_recv, sib_id)

    def c_flow(op):
        for i in range(1, 4):
            op(cpart, call.at[x], c_send.at[i - 1], c_recv, x_peer(i))

    def dq_flow(op, mm):
        for k in range(2):
            op(dqb.at[mm, k], dq_out.at[0, :, lanes(att_h)], dq_send.at[mm * 2 + k], dq_recv,
               (8 * (2 * r + k) + mm, x, att_w))

    def dkv_flow(op, j):
        op(dkf.at[0, j], dk_out.at[0, :, lanes(att_h)], dk_send.at[j], dk_recv, (16 * r + j, x, att_w))
        op(dkf.at[1, j], dv_out.at[0, :, lanes(att_h)], dv_send.at[j], dv_recv, (16 * r + j, x, att_w))

    def fw_flow(op):
        part = kv.at[pl.ds(16 * r, 16), pl.ds(0, 144)]
        op(part, part, fw_send, fw_recv, sib_id)

    spill_copy = remote(gext.at[pl.ds(64, 8)], spill_in, sp_send, sp_recv, (s - 1, x, r))
    row_copy = remote(lrow, prow, lr_send, lr_recv, (s + 1, x, r))
    ex_copy = remote(acc.at[1 - r], sib, ex_send, ex_recv, sib_id)

    barrier = pltpu.get_barrier_semaphore()

    def greet(t):
        @pl.when(jnp.logical_not(same(t)))
        def _():
            pl.semaphore_signal(barrier, inc=1, device_id=t, device_id_type=MESH)

    for h in range(NH):
        for c in range(2):
            greet((att_seq(h, r), x, c))
    for i in range(1, 4):
        greet(y_peer(i))
        greet(x_peer(i))
    for i in (1, 2, 6, 7):
        greet(z_peer(i))
    for i in range(4):
        greet((4 * z + i, y, r))
        greet((4 * z + x, i, r))
    greet(sib_id)

    @pl.when(s > 0)
    def _():
        greet((s - 1, x, r))

    @pl.when(s < NS - 1)
    def _():
        greet((s + 1, x, r))

    @pl.when(is_att)
    def _():
        def one(j, _):
            greet((j, x, att_w))
            return 0

        lax.fori_loop(0, NS, one, 0)

    start_row = starts[...].astype(F32)
    before = lax.broadcasted_iota(jnp.int32, (NB, NB), 0) <= lax.broadcasted_iota(jnp.int32, (NB, NB), 1)
    tri = jnp.where(before, 1.0, 0.0).astype(BF16)
    rank = nn(jnp.broadcast_to(start_row, (16, NB)).astype(BF16), tri)[0:1] - 1.0
    count = jnp.sum(start_row, axis=1, keepdims=True)
    slot80 = lax.broadcasted_iota(jnp.int32, (80, NB), 0).astype(F32)
    want = jnp.where(slot80 < 64.0, slot80, jnp.where(slot80 == 64.0, -1.0, -2.0))
    sel = jnp.where(jnp.broadcast_to(rank, (80, NB)) == want, 1.0, 0.0)
    sel_s[...] = sel
    weight = sel * conf[...]
    w_hi = weight.astype(BF16)
    w_lo = (weight - w_hi.astype(F32)).astype(BF16)
    upstream = up[0]
    gext[...] = nn(w_hi, upstream) + nn(w_lo, upstream)
    for h in range(NH):
        cols = slice(h * HEAD_DIM, (h + 1) * HEAD_DIM)
        stage[h, 0:64] = k_in[0, :, cols]
        stage[h, 64:128] = v_in[0, :, cols]
        stage[h, 128:144] = jnp.broadcast_to(count, (16, HEAD_DIM)).astype(BF16)
        stage[h, 144:208] = q_in[0, :, cols]
    picked = sel[0:64] * start_row
    picked_t = picked.T.astype(BF16)
    grows[...] = nn(picked.astype(BF16), states[0])
    wq[z, mine48] = w_in[mine48]
    last = lax.broadcasted_iota(jnp.int32, (64, D), 0).astype(F32) == count - 1.0
    place = lax.broadcasted_iota(jnp.int32, (1, 1024), 1)
    group, at = lax.div(place, 256), lax.rem(place, 256)
    source = jnp.where(at < 96, 96 * group + at, jnp.where(at < 192, 96 * group + 288 + at, -1))
    perm[...] = jnp.where(lax.broadcasted_iota(jnp.int32, (D, 1024), 0) == source, 1.0, 0.0).astype(BF16)
    packed = jnp.where(at < 192, 192 * group + at, -1)
    pack[...] = jnp.where(lax.broadcasted_iota(jnp.int32, (D, 1024), 0) == packed, 1.0, 0.0).astype(BF16)

    @pl.when(s == NS - 1)
    def _():
        spill_in[...] = jnp.zeros_like(spill_in)

    @pl.when(s == 0)
    def _():
        prow[...] = jnp.zeros_like(prow)

    partners = (
        12 + 3 + 3 + 4 + 8 + 1
        - jnp.where(x == y, 2, 0)
        + jnp.where(s > 0, 1, 0) + jnp.where(s < NS - 1, 1, 0)
        + jnp.where(is_att, jnp.where(att_w == r, 30, 32), 0)
    )
    pl.semaphore_wait(barrier, partners)

    @pl.when(s > 0)
    def _():
        spill_copy.start()

    kv_flow(send)
    wa_flow(start)

    @pl.when(s < NS - 1)
    def _():
        spill_copy.wait_recv()

    group_grad = gext[0:64] + jnp.where(last, spill_in[0:1], 0.0)
    g_hi = group_grad.astype(BF16)
    spread = nn(g_hi, perm[...]).astype(BF16)
    for i in range(4):
        gp[i] = spread[:, 256 * i:256 * (i + 1)]
    g_flow(send)
    g_lo = (group_grad - g_hi.astype(F32)).astype(BF16)
    byte_grad[0] = (upstream.astype(F32) + nn(picked_t, g_hi) + nn(picked_t, g_lo)).astype(BF16)

    landed(gr, g_recv)
    gathered = jnp.concatenate([gr[0], gr[1], gr[2], gr[3]], axis=1)
    gq[x] = nt(gathered, pack[...]).astype(BF16)
    gx_flow(start)
    for j in (2, 3):
        landed(w_in.at[pl.ds(0, 48)], wa_recv.at[j])
    wb_flow(start)

    @pl.when(is_att)
    def _():
        landed(kv.at[pl.ds(16 * r, 16)], kv_recv)
        fw_flow(start)
        landed(kv.at[pl.ds(0, 16), pl.ds(0, 144)], fw_recv)
        kt[...] = kv[:, 0:64, :].reshape(2048, HEAD_DIM).T
        vt[...] = kv[:, 64:128, :].reshape(2048, HEAD_DIM).T
        lane = lax.broadcasted_iota(jnp.int32, (1, 128), 1).astype(F32)
        for p in range(16):
            c0 = kv[2 * p, 128:144, :].astype(F32)[0:1]
            c1 = kv[2 * p + 1, 128:144, :].astype(F32)[0:1]
            live = jnp.where(lane < 64.0, jnp.where(lane < c0, 1.0, 0.0), jnp.where(lane - 64.0 < c1, 1.0, 0.0))
            row = jnp.where(live > 0.0, lane + 128.0 * p, FAR_KEY)
            kkb[:, p * 128:(p + 1) * 128] = jnp.broadcast_to(row, (8, 128))

        def forward(step, _):
            i = lax.rem(step + att, 4)
            slot = lax.broadcasted_iota(jnp.int32, (64, 128), 0).astype(F32)
            places, queries = [], []
            for mm in range(2):
                for k in range(2):
                    block = 8 * (2 * r + k) + 2 * i + mm
                    cnt = kv[block, 128:144, :].astype(F32)[0:1]
                    base = (block * 64).astype(F32)
                    places.append(jnp.where(slot < cnt, slot + base, FAR_QUERY))
                    queries.append(kv[block, 144:208, :])
            place = jnp.concatenate(places, axis=0)
            place = jnp.concatenate([place] * 16, axis=1)
            scores = nn(jnp.concatenate(queries, axis=0), kt[...])
            scores = jnp.where(jnp.broadcast_to(kkb[0:1], (256, 2048)) <= place, scores, -jnp.inf)
            top = jnp.max(scores, axis=1, keepdims=True)
            attention = jnp.exp2((scores - top) * SCALE_LOG2E)
            total = jnp.sum(attention, axis=1, keepdims=True)
            rounded = attention.astype(BF16)
            probs[i] = rounded
            inverse = 1.0 / total
            inv[i] = jnp.broadcast_to(inverse, (256, HEAD_DIM))
            out = nn(rounded, kv[:, 64:128, :].reshape(2048, HEAD_DIM)) * inverse
            a_out[pl.ds(2 * i, 2)] = out.astype(BF16).reshape(2, 2, 64, HEAD_DIM)
            a_flow(send, 2 * i)
            a_flow(send, 2 * i + 1)
            return 0

        lax.fori_loop(0, 4, forward, 0)

    for j in (0, 1):
        landed(w_in.at[pl.ds(0, 48)], wa_recv.at[j])
    landed(wq.at[pl.ds(0, 3), pl.ds(0, 48)], wb_recv)
    wd_flow(start)
    landed(gq.at[pl.ds(0, 3)], gx_recv)
    landed(wq.at[:, pl.ds(0, 48)], wd_recv)

    g_all = gq[...].reshape(256, D)
    w_all = wq[...].reshape(D, D)
    dop[...] = nn(g_all, w_all).astype(BF16).reshape(4, 64, D)
    dr_flow(start)
    landed(w_in.at[pl.ds(0, 64)], a_recv)
    ay_flow(start)

    landed(dr.at[pl.ds(0, 3)], dr_recv)
    dr[y] = dop[y]
    og[...] = (dr[0].astype(F32) + dr[1].astype(F32) + dr[2].astype(F32) + dr[3].astype(F32)).astype(BF16)
    do_flow(send)

    landed(ab.at[pl.ds(0, 3)], ay_recv)
    a_all = ab[...].reshape(256, D)
    pp[...] = nt(a_all, wq[...].reshape(D, D)).astype(BF16).reshape(4, 64, D)
    px_flow(start)
    wgp[...] = nn(gq[...].reshape(256, D).T, a_all).reshape(8, 96, D)
    wgs[...] = wgp[:, pl.ds(pl.multiple_of(48 * (1 - r), 16), 48)].astype(BF16)
    w0_flow(start)


    landed(wg0, w0_recv)
    wh[...] = (wgp[:, mine48] + wg0[...].astype(F32)).astype(BF16)
    w1_flow(start)

    landed(p1.at[pl.ds(0, 3)], px_recv)
    p1[x] = pp[x]
    summed = (p1[0].astype(F32) + p1[1].astype(F32) + p1[2].astype(F32) + p1[3].astype(F32)).astype(BF16)
    apart = nn(summed, pack[...]).astype(BF16)
    for i in range(4):
        ps4[i] = apart[:, 256 * i:256 * (i + 1)]
    p_flow(send)

    for j in range(3):
        landed(rl.at[j], rl_recv.at[j])
    far = rl[2].astype(F32)
    rs[0] = (wh[z_place(2)].astype(F32) + rl[0].astype(F32) + jnp.where(even, far, 0.0)).astype(BF16)
    rs[1] = (wh[z_place(6)].astype(F32) + rl[1].astype(F32) + jnp.where(even, 0.0, far)).astype(BF16)
    w2_flow(start)

    @pl.when(is_att)
    def _():
        landed(dob, do_recv)
        acc[...] = jnp.zeros_like(acc)

        def backward(step, _):
            i = lax.rem(step + att, 4)
            queries = jnp.concatenate(
                [kv[8 * (2 * r + k) + 2 * i + mm, 144:208, :] for mm in range(2) for k in range(2)], axis=0)
            grad = dob[pl.ds(2 * i, 2)].reshape(256, HEAD_DIM).astype(F32)
            grad = (grad * inv[i]).astype(BF16)
            attended = a_out[pl.ds(2 * i, 2)].reshape(256, HEAD_DIM)
            dots = jnp.sum(grad.astype(F32) * attended.astype(F32), axis=1, keepdims=True)
            flow = nn(grad, vt[...])
            weights = probs[i]
            dscore = (weights.astype(F32) * (flow - dots)).astype(BF16)
            dq = nn(dscore, kv[:, 0:64, :].reshape(2048, HEAD_DIM)) * SCALE
            dqb[pl.ds(2 * i, 2)] = dq.astype(BF16).reshape(2, 2, 64, HEAD_DIM)
            dq_flow(send, 2 * i)
            dq_flow(send, 2 * i + 1)
            dk = nn(queries.T, dscore)
            dv = nn(grad.T, weights)
            for c in range(2):
                cols = slice(1024 * c, 1024 * (c + 1))
                acc[c, 0] += dk[:, cols]
                acc[c, 1] += dv[:, cols]
            return 0

        lax.fori_loop(0, 4, backward, 0)
        ex_copy.start()
        ex_copy.wait_recv()
        dkf[0] = ((acc[r, 0] + sib[0]) * SCALE).T.astype(BF16).reshape(16, 64, HEAD_DIM)
        dkf[1] = (acc[r, 1] + sib[1]).T.astype(BF16).reshape(16, 64, HEAD_DIM)

        def out(step, _):
            dkv_flow(send, lax.rem(step + 3 * att, 16))
            return 0

        lax.fori_loop(0, 16, out, 0)
    landed(pr, p_recv)
    gathered = jnp.concatenate([pr[0], pr[1], pr[2], pr[3]], axis=1)
    group_out = (grows[...] + nt(gathered, perm[...])).astype(BF16)
    lrow[...] = jnp.broadcast_to(
        jnp.sum(jnp.where(last, group_out.astype(F32), 0.0), axis=0, keepdims=True), (16, D)
    ).astype(BF16)

    @pl.when(s < NS - 1)
    def _():
        row_copy.start()

    @pl.when(s > 0)
    def _():
        row_copy.wait_recv()

    rows = jnp.concatenate([group_out, prow[...]], axis=0)
    cross = nt(rows, up[0])
    part = jnp.sum(sel_s[...] * cross, axis=0, keepdims=True)
    cpart[...] = jnp.broadcast_to(part, (8, NB))
    call[x] = cpart[...]
    c_flow(start)
    total_w = wh[z].astype(F32)
    for j in range(4):
        landed(wg1.at[j], w1_recv.at[j])
        total_w = total_w + wg1[j].astype(F32)
    wsum[...] = total_w
    ws_flow(start)
    wg_out[mine48] = wsum[...]

    landed(call.at[pl.ds(0, 3)], c_recv)
    conf_grad[...] = (call[0] + call[1] + call[2] + call[3])[0:1]

    landed(wsum, ws_recv)
    kv_flow(sent)
    g_flow(sent)
    do_flow(sent)
    p_flow(sent)
    for flow in (wa_flow, wb_flow, wd_flow, gx_flow, dr_flow, ay_flow, px_flow, w0_flow, w1_flow, w2_flow, ws_flow, c_flow):
        flow(finish)

    @pl.when(s > 0)
    def _():
        spill_copy.wait_send()

    @pl.when(s < NS - 1)
    def _():
        row_copy.wait_send()

    @pl.when(is_att)
    def _():
        fw_flow(finish)
        ex_copy.wait_send()

        def one(j, _):
            a_flow(sent, j)
            dq_flow(sent, j)
            return 0

        lax.fori_loop(0, 8, one, 0)

        def two(j, _):
            dkv_flow(sent, j)
            return 0

        lax.fori_loop(0, 16, two, 0)

    landed(dq_out, dq_recv)
    landed(dk_out, dk_recv)
    landed(dv_out, dv_recv)


def hand_over(*refs):
    held, sems = refs[12:18], refs[18]
    come = [pltpu.make_async_copy(refs[i], held[i], sems.at[i]) for i in range(6)]
    leave = [pltpu.make_async_copy(held[i], refs[6 + i], sems.at[6 + i]) for i in range(6)]
    for copy in come:
        copy.start()
    for i in range(6):
        come[i].wait()
        leave[i].start()
    for copy in leave:
        copy.wait()


def local(byte_states, boundary, confidence, query_rows, key_rows, value_rows, out_weight, upstream):
    vmem = pl.BlockSpec(memory_space=pltpu.VMEM)
    dma = pltpu.SemaphoreType.DMA
    rows = jax.ShapeDtypeStruct((1, CAP, D), BF16)
    shapes = (
        jax.ShapeDtypeStruct((1, NB, D), BF16),
        jax.ShapeDtypeStruct((1, NB), F32),
        rows, rows, rows,
        jax.ShapeDtypeStruct((96, D), F32),
    )
    parts = pl.pallas_call(
        kernel,
        out_shape=shapes,
        in_specs=[vmem] * 8,
        out_specs=(vmem,) * 6,
        scratch_shapes=[
            pltpu.VMEM((NH, 208, 128), BF16),
            pltpu.VMEM((NS, 208, 128), BF16),
            pltpu.VMEM((8, 96, D), BF16),
            pltpu.VMEM((80, D), F32),
            pltpu.VMEM((8, D), F32),
            pltpu.VMEM((D, 1024), BF16),
            pltpu.VMEM((D, 1024), BF16),
            pltpu.VMEM((4, 64, 256), BF16),
            pltpu.VMEM((4, 64, 256), BF16),
            pltpu.VMEM((4, 64, D), BF16),
            pltpu.VMEM((4, 64, D), BF16),
            pltpu.VMEM((4, 64, D), BF16),
            pltpu.VMEM((64, D), BF16),
            pltpu.VMEM((8, 2, 64, 128), BF16),
            pltpu.VMEM((128, 2048), BF16),
            pltpu.VMEM((128, 2048), BF16),
            pltpu.VMEM((8, 2048), F32),
            pltpu.VMEM((4, 256, 2048), BF16),
            pltpu.VMEM((4, 256, 128), F32),
            pltpu.VMEM((8, 2, 64, 128), BF16),
            pltpu.VMEM((4, 64, D), BF16),
            pltpu.VMEM((4, 64, D), BF16),
            pltpu.VMEM((4, 64, D), BF16),
            pltpu.VMEM((4, 64, 256), BF16),
            pltpu.VMEM((4, 64, 256), BF16),
            pltpu.VMEM((8, 96, D), F32),
            pltpu.VMEM((8, 48, D), BF16),
            pltpu.VMEM((8, 48, D), BF16),
            pltpu.VMEM((8, 48, D), BF16),
            pltpu.VMEM((4, 48, D), BF16),
            pltpu.VMEM((3, 48, D), BF16),
            pltpu.VMEM((2, 48, D), BF16),
            pltpu.VMEM((48, D), F32),
            pltpu.VMEM((16, D), BF16),
            pltpu.VMEM((16, D), BF16),
            pltpu.VMEM((8, NB), F32),
            pltpu.VMEM((4, 8, NB), F32),
            pltpu.VMEM((8, 2, 64, 128), BF16),
            pltpu.VMEM((2, 2, 128, 1024), F32),
            pltpu.VMEM((2, 128, 1024), F32),
            pltpu.VMEM((2, 16, 64, 128), BF16),
            pltpu.VMEM((80, NB), F32),
            pltpu.VMEM((64, D), F32),
            dma((6,)), dma,
            dma, dma,
            dma((4,)), dma((4,)),
            dma((3,)), dma,
            dma, dma,
            dma, dma,
            dma((4,)), dma,
            dma((3,)), dma,
            dma((3,)), dma,
            dma((6,)), dma,
            dma((16,)), dma,
            dma((3,)), dma,
            dma((3,)), dma,
            dma((4,)), dma,
            dma, dma,
            dma((4,)), dma((4,)),
            dma((3,)), dma((3,)),
            dma, dma,
            dma, dma,
            dma((3,)), dma,
            dma((16,)), dma,
            dma((16,)), dma,
            dma((16,)), dma,
            dma, dma,
        ],
        compiler_params=pltpu.CompilerParams(
            collective_id=0, has_side_effects=True, vmem_limit_bytes=56 * 1024 * 1024
        ),
        cost_estimate=pl.CostEstimate(flops=8_000_000_000, bytes_accessed=20_000_000, transcendentals=3_000_000),
    )(byte_states, boundary, confidence, query_rows, key_rows, value_rows, out_weight, upstream)
    whole = pl.BlockSpec(memory_space=pl.ANY)
    return pl.pallas_call(
        hand_over,
        out_shape=shapes,
        in_specs=[whole] * 6,
        out_specs=(whole,) * 6,
        scratch_shapes=[pltpu.VMEM(shape.shape, shape.dtype) for shape in shapes] + [dma((12,))],
        compiler_params=pltpu.CompilerParams(vmem_limit_bytes=60 * 1024 * 1024),
    )(*parts)


def solution(mesh):
    split = P("rep", "seq", "head")
    bytes_ = P("rep", "seq")
    return jax.shard_map(
        local,
        mesh=mesh,
        in_specs=(split, bytes_, bytes_, split, split, split, P("seq", "head"), split),
        out_specs=(split, bytes_, split, split, split, P("seq", "head")),
        check_vma=False,
    )
```

```python
import jax
import jax.numpy as jnp
from jax import lax
from jax.experimental import pallas as pl
from jax.experimental.pallas import tpu as pltpu
from jax.sharding import PartitionSpec as P

MESH = pl.DeviceIdType.MESH
F32, BF16 = jnp.float32, jnp.bfloat16

HEAD_DIM = 128
NS = 32
NH = 6
D = 768
CAP = 64
NB = 256
SCALE = HEAD_DIM ** -0.5
SCALE_LOG2E = SCALE * 1.4426950408889634
FAR_QUERY = 4096.0
FAR_KEY = 8192.0


def att_seq(h, w):
    return lax.div((2 * h + w) * 8, 3)


def nt(a, b):
    return lax.dot_general(a, b, (((1,), (1,)), ((), ())), preferred_element_type=F32)


def nn(a, b):
    return jnp.dot(a, b, preferred_element_type=F32)


def kernel(
    states_h, starts, conf, q_h, k_h, v_h, w_h, up_h,
    byte_out, conf_grad, dq_out, dkv, wg_out,
    states, q_in, k_in, v_in, w_in, up, byte_grad, in_sems, out_sems,
    stage, kv, wq, gext, spill_in, perm, pack, gp, gr, gq, dop, dr, og, dob,
    kt, vt, kkb, probs, inv, a_out, ab, pp, p1, ps4, pr, wgp, wgs, wg0, wh, wg1, rl, rs, wsum,
    lrow, prow, cpart, call, dqb, acc, sib, dkf, sel_s, grows,
    kv_send, kv_recv, fw_send, fw_recv, wa_send, wa_recv, wb_send, wb_recv, wd_send, wd_recv,
    sp_send, sp_recv, g_send, g_recv, gx_send, gx_recv, dr_send, dr_recv,
    do_send, do_recv, a_send, a_recv, ay_send, ay_recv, px_send, px_recv, p_send, p_recv,
    w0_send, w0_recv, w1_send, w1_recv, rl_send, rl_recv, ws_send, ws_recv,
    lr_send, lr_recv, c_send, c_recv, dq_send, dq_recv, dk_send, dk_recv,
    ex_send, ex_recv,
):
    s = lax.axis_index("seq")
    x = lax.axis_index("head")
    r = lax.axis_index("rep")
    q = lax.div(s, 8)
    m = lax.rem(s, 8)
    z = lax.div(s, 4)
    y = lax.rem(m, 4)
    half = lax.div(q, 2)
    att = lax.div(3 * s + 7, 8)
    is_att = jnp.logical_and(lax.div(att * 8, 3) == s, att < 12)
    att_h = lax.div(att, 2)
    att_w = lax.rem(att, 2)

    def same(t):
        return jnp.logical_and(jnp.logical_and(t[0] == s, t[1] == x), t[2] == r)

    def send(src, dst, ssem, rsem, t):
        mine = same(t)

        @pl.when(jnp.logical_not(mine))
        def _():
            pltpu.make_async_remote_copy(src, dst, ssem, rsem, device_id=t, device_id_type=MESH).start()

        @pl.when(mine)
        def _():
            pltpu.make_async_copy(src, dst, rsem).start()

    def sent(src, dst, ssem, rsem, t):
        @pl.when(jnp.logical_not(same(t)))
        def _():
            pltpu.make_async_remote_copy(src, dst, ssem, rsem, device_id=t, device_id_type=MESH).wait_send()

    def landed(ref, rsem):
        pltpu.make_async_copy(ref, ref, rsem).wait()

    def remote(src, dst, ssem, rsem, t):
        return pltpu.make_async_remote_copy(src, dst, ssem, rsem, device_id=t, device_id_type=MESH)

    def start(*a):
        remote(*a).start()

    def finish(*a):
        remote(*a).wait_send()

    def lanes(h):
        return pl.ds(h * HEAD_DIM if isinstance(h, int) else pl.multiple_of(h * HEAD_DIM, HEAD_DIM), HEAD_DIM)

    mine48 = pl.ds(pl.multiple_of(48 * r, 16), 48)
    sib_id = (s, x, 1 - r)

    def y_peer(i):
        return (s - y + lax.rem(y + i, 4), x, r)

    def z_place(i):
        return lax.rem(z + i, 8)

    def z_peer(i):
        return (4 * z_place(i) + y, x, r)

    def x_peer(i):
        return (s, lax.rem(x + i, 4), r)

    def kv_flow(op):
        for i in range(NH):
            h = lax.rem(s + 3 * r + i, NH)
            op(stage.at[h], kv.at[s], kv_send.at[i], kv_recv, (att_seq(h, r), x, half))

    even = lax.rem(z, 2) == 0

    def wa_flow(op):
        for j, i in enumerate((1, 7, 2, 6)):
            op(w_in.at[mine48], wq.at[z, mine48], wa_send.at[j], wa_recv.at[j], z_peer(i))

    def wb_flow(op):
        for j, (block, i) in enumerate(((6, 1), (2, 7), (jnp.where(even, 6, 2), jnp.where(even, 2, 6)))):
            part = wq.at[z_place(block), mine48]
            op(part, part, wb_send.at[j], wb_recv, z_peer(i))

    def wd_flow(op):
        op(wq.at[:, mine48], wq.at[:, mine48], wd_send, wd_recv, sib_id)

    def g_flow(op):
        for i in range(4):
            op(gp.at[i], gr.at[x], g_send.at[i], g_recv, (4 * z + i, y, r))

    def gx_flow(op):
        for i in range(1, 4):
            op(gq.at[x], gq.at[x], gx_send.at[i - 1], gx_recv, x_peer(i))

    def dr_flow(op):
        for i in range(1, 4):
            op(dop.at[lax.rem(y + i, 4)], dr.at[y], dr_send.at[i - 1], dr_recv, y_peer(i))

    def do_flow(op):
        for i in range(NH):
            h = lax.rem(s + 3 * r + i, NH)
            op(og.at[:, lanes(h)], dob.at[m, lax.rem(q, 2)], do_send.at[i], do_recv, (att_seq(h, r), x, half))

    def a_flow(op, mm):
        for k in range(2):
            op(a_out.at[mm, k], ab.at[lax.rem(mm, 4), :, lanes(att_h)], a_send, a_recv,
               (8 * (2 * r + k) + mm, x, att_w))

    def ay_flow(op):
        for i in range(1, 4):
            op(ab.at[y], ab.at[y], ay_send.at[i - 1], ay_recv, y_peer(i))

    def px_flow(op):
        for i in range(1, 4):
            op(pp.at[lax.rem(x + i, 4)], p1.at[x], px_send.at[i - 1], px_recv, x_peer(i))

    def p_flow(op):
        for i in range(4):
            op(ps4.at[i], pr.at[y], p_send.at[i], p_recv, (4 * z + x, i, r))

    def w0_flow(op):
        op(wgs, wg0, w0_send, w0_recv, sib_id)

    def w1_flow(op):
        for j, i in enumerate((1, 7)):
            op(wh.at[z_place(i)], wg1.at[j], w1_send.at[j], w1_recv.at[j], z_peer(i))
        for j, (block, i) in enumerate(((3, 1), (5, 7), (4, jnp.where(even, 2, 6)))):
            op(wh.at[z_place(block)], rl.at[j], rl_send.at[j], rl_recv.at[j], z_peer(i))

    def w2_flow(op):
        for j, i in enumerate((2, 6)):
            op(rs.at[j], wg1.at[2 + j], w1_send.at[2 + j], w1_recv.at[2 + j], z_peer(i))

    def ws_flow(op):
        op(wsum, wg_out.at[mine48], ws_send, ws_recv, sib_id)

    def c_flow(op):
        for i in range(1, 4):
            op(cpart, call.at[x], c_send.at[i - 1], c_recv, x_peer(i))

    def dq_flow(op, mm):
        for k in range(2):
            op(dqb.at[mm, k], dq_out.at[0, :, lanes(att_h)], dq_send, dq_recv,
               (8 * (2 * r + k) + mm, x, att_w))

    def dkv_flow(op, j):
        op(dkf.at[j], dkv.at[:, :, lanes(att_h)], dk_send, dk_recv, (16 * r + j, x, att_w))

    def fw_flow(op):
        part = kv.at[pl.ds(16 * r, 16), pl.ds(0, 144)]
        op(part, part, fw_send, fw_recv, sib_id)

    spill_copy = remote(gext.at[pl.ds(64, 8)], spill_in, sp_send, sp_recv, (s - 1, x, r))
    row_copy = remote(lrow, prow, lr_send, lr_recv, (s + 1, x, r))
    ex_copy = remote(acc.at[1 - r], sib, ex_send, ex_recv, sib_id)

    loads = [
        pltpu.make_async_copy(there, here, in_sems.at[i])
        for i, (there, here) in enumerate(
            ((k_h, k_in), (v_h, v_in), (q_h, q_in), (w_h, w_in), (up_h, up), (states_h, states)))
    ]
    for load in loads:
        load.start()

    barrier = pltpu.get_barrier_semaphore()

    def greet(t):
        @pl.when(jnp.logical_not(same(t)))
        def _():
            pl.semaphore_signal(barrier, inc=1, device_id=t, device_id_type=MESH)

    for h in range(NH):
        for c in range(2):
            greet((att_seq(h, r), x, c))
    for i in range(1, 4):
        greet(y_peer(i))
        greet(x_peer(i))
    for i in (1, 2, 6, 7):
        greet(z_peer(i))
    for i in range(4):
        greet((4 * z + i, y, r))
        greet((4 * z + x, i, r))
    greet(sib_id)

    @pl.when(s > 0)
    def _():
        greet((s - 1, x, r))

    @pl.when(s < NS - 1)
    def _():
        greet((s + 1, x, r))

    @pl.when(is_att)
    def _():
        def one(j, _):
            greet((j, x, att_w))
            return 0

        lax.fori_loop(0, NS, one, 0)

    for load in loads:
        load.wait()
    start_row = starts[...].astype(F32)
    before = lax.broadcasted_iota(jnp.int32, (NB, NB), 0) <= lax.broadcasted_iota(jnp.int32, (NB, NB), 1)
    tri = jnp.where(before, 1.0, 0.0).astype(BF16)
    rank = nn(jnp.broadcast_to(start_row, (16, NB)).astype(BF16), tri)[0:1] - 1.0
    count = jnp.sum(start_row, axis=1, keepdims=True)
    slot80 = lax.broadcasted_iota(jnp.int32, (80, NB), 0).astype(F32)
    want = jnp.where(slot80 < 64.0, slot80, jnp.where(slot80 == 64.0, -1.0, -2.0))
    sel = jnp.where(jnp.broadcast_to(rank, (80, NB)) == want, 1.0, 0.0)
    sel_s[...] = sel
    weight = sel * conf[...]
    w_hi = weight.astype(BF16)
    w_lo = (weight - w_hi.astype(F32)).astype(BF16)
    upstream = up[0]
    gext[...] = nn(w_hi, upstream) + nn(w_lo, upstream)
    for h in range(NH):
        cols = slice(h * HEAD_DIM, (h + 1) * HEAD_DIM)
        stage[h, 0:64] = k_in[0, :, cols]
        stage[h, 64:128] = v_in[0, :, cols]
        stage[h, 128:144] = jnp.broadcast_to(count, (16, HEAD_DIM)).astype(BF16)
        stage[h, 144:208] = q_in[0, :, cols]
    picked = sel[0:64] * start_row
    picked_t = picked.T.astype(BF16)
    grows[...] = nn(picked.astype(BF16), states[0])
    wq[z, mine48] = w_in[mine48]
    last = lax.broadcasted_iota(jnp.int32, (64, D), 0).astype(F32) == count - 1.0
    place = lax.broadcasted_iota(jnp.int32, (1, 1024), 1)
    group, at = lax.div(place, 256), lax.rem(place, 256)
    source = jnp.where(at < 96, 96 * group + at, jnp.where(at < 192, 96 * group + 288 + at, -1))
    perm[...] = jnp.where(lax.broadcasted_iota(jnp.int32, (D, 1024), 0) == source, 1.0, 0.0).astype(BF16)
    packed = jnp.where(at < 192, 192 * group + at, -1)
    pack[...] = jnp.where(lax.broadcasted_iota(jnp.int32, (D, 1024), 0) == packed, 1.0, 0.0).astype(BF16)

    @pl.when(s == NS - 1)
    def _():
        spill_in[...] = jnp.zeros_like(spill_in)

    @pl.when(s == 0)
    def _():
        prow[...] = jnp.zeros_like(prow)

    partners = (
        12 + 3 + 3 + 4 + 8 + 1
        - jnp.where(x == y, 2, 0)
        + jnp.where(s > 0, 1, 0) + jnp.where(s < NS - 1, 1, 0)
        + jnp.where(is_att, jnp.where(att_w == r, 30, 32), 0)
    )
    pl.semaphore_wait(barrier, partners)

    @pl.when(s > 0)
    def _():
        spill_copy.start()

    kv_flow(send)
    wa_flow(start)

    @pl.when(s < NS - 1)
    def _():
        spill_copy.wait_recv()

    group_grad = gext[0:64] + jnp.where(last, spill_in[0:1], 0.0)
    g_hi = group_grad.astype(BF16)
    spread = nn(g_hi, perm[...]).astype(BF16)
    for i in range(4):
        gp[i] = spread[:, 256 * i:256 * (i + 1)]
    g_flow(send)
    g_lo = (group_grad - g_hi.astype(F32)).astype(BF16)
    byte_grad[0] = (upstream.astype(F32) + nn(picked_t, g_hi) + nn(picked_t, g_lo)).astype(BF16)
    byte_copy = pltpu.make_async_copy(byte_grad, byte_out, out_sems.at[0])
    byte_copy.start()

    landed(gr, g_recv)
    gathered = jnp.concatenate([gr[0], gr[1], gr[2], gr[3]], axis=1)
    gq[x] = nt(gathered, pack[...]).astype(BF16)
    gx_flow(start)
    for j in (2, 3):
        landed(w_in.at[pl.ds(0, 48)], wa_recv.at[j])
    wb_flow(start)

    @pl.when(is_att)
    def _():
        landed(kv.at[pl.ds(16 * r, 16)], kv_recv)
        fw_flow(start)
        landed(kv.at[pl.ds(0, 16), pl.ds(0, 144)], fw_recv)
        kt[...] = kv[:, 0:64, :].reshape(2048, HEAD_DIM).T
        vt[...] = kv[:, 64:128, :].reshape(2048, HEAD_DIM).T
        lane = lax.broadcasted_iota(jnp.int32, (1, 128), 1).astype(F32)
        for p in range(16):
            c0 = kv[2 * p, 128:144, :].astype(F32)[0:1]
            c1 = kv[2 * p + 1, 128:144, :].astype(F32)[0:1]
            live = jnp.where(lane < 64.0, jnp.where(lane < c0, 1.0, 0.0), jnp.where(lane - 64.0 < c1, 1.0, 0.0))
            row = jnp.where(live > 0.0, lane + 128.0 * p, FAR_KEY)
            kkb[:, p * 128:(p + 1) * 128] = jnp.broadcast_to(row, (8, 128))

        def forward(step, _):
            i = lax.rem(step + att, 4)
            slot = lax.broadcasted_iota(jnp.int32, (64, 128), 0).astype(F32)
            places, queries = [], []
            for mm in range(2):
                for k in range(2):
                    block = 8 * (2 * r + k) + 2 * i + mm
                    cnt = kv[block, 128:144, :].astype(F32)[0:1]
                    base = (block * 64).astype(F32)
                    places.append(jnp.where(slot < cnt, slot + base, FAR_QUERY))
                    queries.append(kv[block, 144:208, :])
            place = jnp.concatenate(places, axis=0)
            place = jnp.concatenate([place] * 16, axis=1)
            scores = nn(jnp.concatenate(queries, axis=0), kt[...])
            scores = jnp.where(jnp.broadcast_to(kkb[0:1], (256, 2048)) <= place, scores, -jnp.inf)
            top = jnp.max(scores, axis=1, keepdims=True)
            attention = jnp.exp2((scores - top) * SCALE_LOG2E)
            total = jnp.sum(attention, axis=1, keepdims=True)
            rounded = attention.astype(BF16)
            probs[i] = rounded
            inverse = 1.0 / total
            inv[i] = jnp.broadcast_to(inverse, (256, HEAD_DIM))
            out = nn(rounded, kv[:, 64:128, :].reshape(2048, HEAD_DIM)) * inverse
            a_out[pl.ds(2 * i, 2)] = out.astype(BF16).reshape(2, 2, 64, HEAD_DIM)
            a_flow(send, 2 * i)
            a_flow(send, 2 * i + 1)
            return 0

        lax.fori_loop(0, 4, forward, 0)

    for j in (0, 1):
        landed(w_in.at[pl.ds(0, 48)], wa_recv.at[j])
    landed(wq.at[pl.ds(0, 3), pl.ds(0, 48)], wb_recv)
    wd_flow(start)
    landed(gq.at[pl.ds(0, 3)], gx_recv)
    landed(wq.at[:, pl.ds(0, 48)], wd_recv)

    g_all = gq[...].reshape(256, D)
    w_all = wq[...].reshape(D, D)
    dop[...] = nn(g_all, w_all).astype(BF16).reshape(4, 64, D)
    dr_flow(start)
    landed(w_in.at[pl.ds(0, 64)], a_recv)
    ay_flow(start)

    landed(dr.at[pl.ds(0, 3)], dr_recv)
    dr[y] = dop[y]
    og[...] = (dr[0].astype(F32) + dr[1].astype(F32) + dr[2].astype(F32) + dr[3].astype(F32)).astype(BF16)
    do_flow(send)

    landed(ab.at[pl.ds(0, 3)], ay_recv)
    a_all = ab[...].reshape(256, D)
    pp[...] = nt(a_all, wq[...].reshape(D, D)).astype(BF16).reshape(4, 64, D)
    px_flow(start)
    wgp[...] = nn(gq[...].reshape(256, D).T, a_all).reshape(8, 96, D)
    wgs[...] = wgp[:, pl.ds(pl.multiple_of(48 * (1 - r), 16), 48)].astype(BF16)
    w0_flow(start)


    @pl.when(is_att)
    def _():
        landed(dob, do_recv)
        acc[...] = jnp.zeros_like(acc)

        def backward(step, _):
            i = lax.rem(step + att, 4)
            queries = jnp.concatenate(
                [kv[8 * (2 * r + k) + 2 * i + mm, 144:208, :] for mm in range(2) for k in range(2)], axis=0)
            grad = dob[pl.ds(2 * i, 2)].reshape(256, HEAD_DIM).astype(F32)
            grad = (grad * inv[i]).astype(BF16)
            attended = a_out[pl.ds(2 * i, 2)].reshape(256, HEAD_DIM)
            dots = jnp.sum(grad.astype(F32) * attended.astype(F32), axis=1, keepdims=True)
            flow = nn(grad, vt[...])
            weights = probs[i]
            dscore = (weights.astype(F32) * (flow - dots)).astype(BF16)
            dq = nn(dscore, kv[:, 0:64, :].reshape(2048, HEAD_DIM)) * SCALE
            dqb[pl.ds(2 * i, 2)] = dq.astype(BF16).reshape(2, 2, 64, HEAD_DIM)
            dq_flow(send, 2 * i)
            dq_flow(send, 2 * i + 1)
            dk = nn(queries.T, dscore)
            dv = nn(grad.T, weights)
            for c in range(2):
                cols = slice(1024 * c, 1024 * (c + 1))
                acc[c, 0] += dk[:, cols]
                acc[c, 1] += dv[:, cols]
            return 0

        lax.fori_loop(0, 4, backward, 0)
        ex_copy.start()

    landed(wg0, w0_recv)
    wh[...] = (wgp[:, mine48] + wg0[...].astype(F32)).astype(BF16)
    w1_flow(start)

    landed(p1.at[pl.ds(0, 3)], px_recv)
    p1[x] = pp[x]
    summed = (p1[0].astype(F32) + p1[1].astype(F32) + p1[2].astype(F32) + p1[3].astype(F32)).astype(BF16)
    apart = nn(summed, pack[...]).astype(BF16)
    for i in range(4):
        ps4[i] = apart[:, 256 * i:256 * (i + 1)]
    p_flow(send)

    for j in range(3):
        landed(rl.at[j], rl_recv.at[j])
    far = rl[2].astype(F32)
    rs[0] = (wh[z_place(2)].astype(F32) + rl[0].astype(F32) + jnp.where(even, far, 0.0)).astype(BF16)
    rs[1] = (wh[z_place(6)].astype(F32) + rl[1].astype(F32) + jnp.where(even, 0.0, far)).astype(BF16)
    w2_flow(start)

    @pl.when(is_att)
    def _():
        ex_copy.wait_recv()
        dkf[:, 0] = ((acc[r, 0] + sib[0]) * SCALE).T.astype(BF16).reshape(16, 64, HEAD_DIM)
        dkf[:, 1] = (acc[r, 1] + sib[1]).T.astype(BF16).reshape(16, 64, HEAD_DIM)

        def out(step, _):
            dkv_flow(send, lax.rem(step + 3 * att, 16))
            return 0

        lax.fori_loop(0, 16, out, 0)
    landed(pr, p_recv)
    gathered = jnp.concatenate([pr[0], pr[1], pr[2], pr[3]], axis=1)
    group_out = (grows[...] + nt(gathered, perm[...])).astype(BF16)
    lrow[...] = jnp.broadcast_to(
        jnp.sum(jnp.where(last, group_out.astype(F32), 0.0), axis=0, keepdims=True), (16, D)
    ).astype(BF16)

    @pl.when(s < NS - 1)
    def _():
        row_copy.start()

    @pl.when(s > 0)
    def _():
        row_copy.wait_recv()

    rows = jnp.concatenate([group_out, prow[...]], axis=0)
    cross = nt(rows, up[0])
    part = jnp.sum(sel_s[...] * cross, axis=0, keepdims=True)
    cpart[...] = jnp.broadcast_to(part, (8, NB))
    call[x] = cpart[...]
    c_flow(start)
    total_w = wh[z].astype(F32)
    for j in range(4):
        landed(wg1.at[j], w1_recv.at[j])
        total_w = total_w + wg1[j].astype(F32)
    wsum[...] = total_w
    ws_flow(start)
    wg_copy = pltpu.make_async_copy(wsum, wg_out.at[mine48], out_sems.at[1])
    wg_copy.start()

    landed(call.at[pl.ds(0, 3)], c_recv)
    conf_grad[...] = (call[0] + call[1] + call[2] + call[3])[0:1]

    landed(wsum, ws_recv)
    kv_flow(sent)
    g_flow(sent)
    do_flow(sent)
    p_flow(sent)
    for flow in (wa_flow, wb_flow, wd_flow, gx_flow, dr_flow, ay_flow, px_flow, w0_flow, w1_flow, w2_flow, ws_flow, c_flow):
        flow(finish)

    @pl.when(s > 0)
    def _():
        spill_copy.wait_send()

    @pl.when(s < NS - 1)
    def _():
        row_copy.wait_send()

    @pl.when(is_att)
    def _():
        fw_flow(finish)
        ex_copy.wait_send()

        own = jnp.logical_and(att_w == r, half == r)
        for count_of, there in ((15, own), (16, jnp.logical_not(own))):
            @pl.when(there)
            def _(count_of=count_of):
                landed(kv.at[pl.ds(0, count_of), pl.ds(0, 64)], a_send)
                landed(kv.at[pl.ds(0, count_of), pl.ds(0, 64)], dq_send)
                landed(kv.at[pl.ds(0, count_of), pl.ds(0, 128)], dk_send)

    landed(dq_out, dq_recv)
    landed(dkv, dk_recv)
    byte_copy.wait()
    wg_copy.wait()


def hand_over(byte_in, conf_in, dq_in, dkv_in, wg_in, *refs):
    outs, held, sems = refs[:6], refs[6:12], refs[12]
    come = [byte_in, conf_in, dq_in, dkv_in.at[pl.ds(0, 1)], dkv_in.at[pl.ds(1, 1)], wg_in]
    come = [pltpu.make_async_copy(come[i], held[i], sems.at[i]) for i in range(6)]
    leave = [pltpu.make_async_copy(held[i], outs[i], sems.at[6 + i]) for i in range(6)]
    for copy in come:
        copy.start()
    for i in range(6):
        come[i].wait()
        leave[i].start()
    for copy in leave:
        copy.wait()


def local(byte_states, boundary, confidence, query_rows, key_rows, value_rows, out_weight, upstream):
    vmem = pl.BlockSpec(memory_space=pltpu.VMEM)
    whole = pl.BlockSpec(memory_space=pl.ANY)
    dma = pltpu.SemaphoreType.DMA
    rows = jax.ShapeDtypeStruct((1, CAP, D), BF16)
    shapes = (
        jax.ShapeDtypeStruct((1, NB, D), BF16),
        jax.ShapeDtypeStruct((1, NB), F32),
        rows, rows, rows,
        jax.ShapeDtypeStruct((96, D), F32),
    )
    parts = pl.pallas_call(
        kernel,
        out_shape=(*shapes[:3], jax.ShapeDtypeStruct((2, CAP, D), BF16), shapes[5]),
        in_specs=[whole, vmem, vmem] + [whole] * 5,
        out_specs=(whole, vmem, whole, whole, whole),
        scratch_shapes=[
            pltpu.VMEM((1, NB, D), BF16),
            pltpu.VMEM((1, CAP, D), BF16),
            pltpu.VMEM((1, CAP, D), BF16),
            pltpu.VMEM((1, CAP, D), BF16),
            pltpu.VMEM((96, D), BF16),
            pltpu.VMEM((1, NB, D), BF16),
            pltpu.VMEM((1, NB, D), BF16),
            dma((6,)), dma((2,)),
            pltpu.VMEM((NH, 208, 128), BF16),
            pltpu.VMEM((NS, 208, 128), BF16),
            pltpu.VMEM((8, 96, D), BF16),
            pltpu.VMEM((80, D), F32),
            pltpu.VMEM((8, D), F32),
            pltpu.VMEM((D, 1024), BF16),
            pltpu.VMEM((D, 1024), BF16),
            pltpu.VMEM((4, 64, 256), BF16),
            pltpu.VMEM((4, 64, 256), BF16),
            pltpu.VMEM((4, 64, D), BF16),
            pltpu.VMEM((4, 64, D), BF16),
            pltpu.VMEM((4, 64, D), BF16),
            pltpu.VMEM((64, D), BF16),
            pltpu.VMEM((8, 2, 64, 128), BF16),
            pltpu.VMEM((128, 2048), BF16),
            pltpu.VMEM((128, 2048), BF16),
            pltpu.VMEM((8, 2048), F32),
            pltpu.VMEM((4, 256, 2048), BF16),
            pltpu.VMEM((4, 256, 128), F32),
            pltpu.VMEM((8, 2, 64, 128), BF16),
            pltpu.VMEM((4, 64, D), BF16),
            pltpu.VMEM((4, 64, D), BF16),
            pltpu.VMEM((4, 64, D), BF16),
            pltpu.VMEM((4, 64, 256), BF16),
            pltpu.VMEM((4, 64, 256), BF16),
            pltpu.VMEM((8, 96, D), F32),
            pltpu.VMEM((8, 48, D), BF16),
            pltpu.VMEM((8, 48, D), BF16),
            pltpu.VMEM((8, 48, D), BF16),
            pltpu.VMEM((4, 48, D), BF16),
            pltpu.VMEM((3, 48, D), BF16),
            pltpu.VMEM((2, 48, D), BF16),
            pltpu.VMEM((48, D), F32),
            pltpu.VMEM((16, D), BF16),
            pltpu.VMEM((16, D), BF16),
            pltpu.VMEM((8, NB), F32),
            pltpu.VMEM((4, 8, NB), F32),
            pltpu.VMEM((8, 2, 64, 128), BF16),
            pltpu.VMEM((2, 2, 128, 1024), F32),
            pltpu.VMEM((2, 128, 1024), F32),
            pltpu.VMEM((16, 2, 64, 128), BF16),
            pltpu.VMEM((80, NB), F32),
            pltpu.VMEM((64, D), F32),
            dma((6,)), dma,
            dma, dma,
            dma((4,)), dma((4,)),
            dma((3,)), dma,
            dma, dma,
            dma, dma,
            dma((4,)), dma,
            dma((3,)), dma,
            dma((3,)), dma,
            dma((6,)), dma,
            dma, dma,
            dma((3,)), dma,
            dma((3,)), dma,
            dma((4,)), dma,
            dma, dma,
            dma((4,)), dma((4,)),
            dma((3,)), dma((3,)),
            dma, dma,
            dma, dma,
            dma((3,)), dma,
            dma, dma,
            dma, dma,
            dma, dma,
        ],
        compiler_params=pltpu.CompilerParams(
            collective_id=0, has_side_effects=True, vmem_limit_bytes=56 * 1024 * 1024
        ),
        cost_estimate=pl.CostEstimate(flops=8_000_000_000, bytes_accessed=20_000_000, transcendentals=3_000_000),
    )(byte_states, boundary, confidence, query_rows, key_rows, value_rows, out_weight, upstream)
    return pl.pallas_call(
        hand_over,
        out_shape=shapes,
        in_specs=[whole] * 5,
        out_specs=(whole,) * 6,
        scratch_shapes=[pltpu.VMEM(shape.shape, shape.dtype) for shape in shapes] + [dma((12,))],
        compiler_params=pltpu.CompilerParams(vmem_limit_bytes=60 * 1024 * 1024),
    )(*parts)


def solution(mesh):
    split = P("rep", "seq", "head")
    bytes_ = P("rep", "seq")
    return jax.shard_map(
        local,
        mesh=mesh,
        in_specs=(split, bytes_, bytes_, split, split, split, P("seq", "head"), split),
        out_specs=(split, bytes_, split, split, split, P("seq", "head")),
        check_vma=False,
    )
```

```python
import jax
import jax.numpy as jnp
from jax import lax
from jax.experimental import pallas as pl
from jax.experimental.pallas import tpu as pltpu
from jax.sharding import PartitionSpec as P

MESH = pl.DeviceIdType.MESH
F32, BF16 = jnp.float32, jnp.bfloat16

HEAD_DIM = 128
NS = 32
NH = 6
D = 768
CAP = 64
NB = 256
SCALE = HEAD_DIM ** -0.5
SCALE_LOG2E = SCALE * 1.4426950408889634
FAR_QUERY = 4096.0
FAR_KEY = 8192.0


def att_seq(h, w):
    return lax.div((2 * h + w) * 8, 3)


def nt(a, b):
    return lax.dot_general(a, b, (((1,), (1,)), ((), ())), preferred_element_type=F32)


def nn(a, b):
    return jnp.dot(a, b, preferred_element_type=F32)


def kernel(
    states, starts, conf, q_in, k_in, v_in, w_in, up,
    byte_grad, conf_grad, dq_out, dk_out, dv_out, wg_out,
    stage, kv, wq, gext, spill_in, perm, pack, gp, gr, gq, dop, dr, og, dob,
    kt, vt, kkb, probs, inv, a_out, ab, pp, p1, ps4, pr, wgp, wgs, wg0, wh, wg1, rl, rs, wsum,
    lrow, prow, cpart, call, dqb, acc, sib, dkf, dkv, sel_s, grows,
    kv_send, kv_recv, fw_send, fw_recv, wa_send, wa_recv, wb_send, wb_recv, wd_send, wd_recv,
    sp_send, sp_recv, g_send, g_recv, gx_send, gx_recv, dr_send, dr_recv,
    do_send, do_recv, a_send, a_recv, ay_send, ay_recv, px_send, px_recv, p_send, p_recv,
    w0_send, w0_recv, w1_send, w1_recv, rl_send, rl_recv, ws_send, ws_recv,
    lr_send, lr_recv, c_send, c_recv, dq_send, dq_recv, dk_send, dk_recv,
    ex_send, ex_recv,
):
    s = lax.axis_index("seq")
    x = lax.axis_index("head")
    r = lax.axis_index("rep")
    q = lax.div(s, 8)
    m = lax.rem(s, 8)
    z = lax.div(s, 4)
    y = lax.rem(m, 4)
    half = lax.div(q, 2)
    att = lax.div(3 * s + 7, 8)
    is_att = jnp.logical_and(lax.div(att * 8, 3) == s, att < 12)
    att_h = lax.div(att, 2)
    att_w = lax.rem(att, 2)

    def same(t):
        return jnp.logical_and(jnp.logical_and(t[0] == s, t[1] == x), t[2] == r)

    def send(src, dst, ssem, rsem, t):
        mine = same(t)

        @pl.when(jnp.logical_not(mine))
        def _():
            pltpu.make_async_remote_copy(src, dst, ssem, rsem, device_id=t, device_id_type=MESH).start()

        @pl.when(mine)
        def _():
            pltpu.make_async_copy(src, dst, rsem).start()

    def sent(src, dst, ssem, rsem, t):
        @pl.when(jnp.logical_not(same(t)))
        def _():
            pltpu.make_async_remote_copy(src, dst, ssem, rsem, device_id=t, device_id_type=MESH).wait_send()

    def landed(ref, rsem):
        pltpu.make_async_copy(ref, ref, rsem).wait()

    def remote(src, dst, ssem, rsem, t):
        return pltpu.make_async_remote_copy(src, dst, ssem, rsem, device_id=t, device_id_type=MESH)

    def start(*a):
        remote(*a).start()

    def finish(*a):
        remote(*a).wait_send()

    def lanes(h):
        return pl.ds(h * HEAD_DIM if isinstance(h, int) else pl.multiple_of(h * HEAD_DIM, HEAD_DIM), HEAD_DIM)

    mine48 = pl.ds(pl.multiple_of(48 * r, 16), 48)
    sib_id = (s, x, 1 - r)

    def y_peer(i):
        return (s - y + lax.rem(y + i, 4), x, r)

    def z_place(i):
        return lax.rem(z + i, 8)

    def z_peer(i):
        return (4 * z_place(i) + y, x, r)

    def x_peer(i):
        return (s, lax.rem(x + i, 4), r)

    def kv_flow(op):
        for i in range(NH):
            h = lax.rem(s + 3 * r + i, NH)
            op(stage.at[h], kv.at[s], kv_send.at[i], kv_recv, (att_seq(h, r), x, half))

    even = lax.rem(z, 2) == 0

    def wa_flow(op):
        for j, i in enumerate((1, 7, 2, 6)):
            op(w_in.at[mine48], wq.at[z, mine48], wa_send.at[j], wa_recv.at[j], z_peer(i))

    def wb_flow(op):
        for j, (block, i) in enumerate(((6, 1), (2, 7), (jnp.where(even, 6, 2), jnp.where(even, 2, 6)))):
            part = wq.at[z_place(block), mine48]
            op(part, part, wb_send.at[j], wb_recv, z_peer(i))

    def wd_flow(op):
        op(wq.at[:, mine48], wq.at[:, mine48], wd_send, wd_recv, sib_id)

    def g_flow(op):
        for i in range(4):
            op(gp.at[i], gr.at[x], g_send.at[i], g_recv, (4 * z + i, y, r))

    def gx_flow(op):
        for i in range(1, 4):
            op(gq.at[x], gq.at[x], gx_send.at[i - 1], gx_recv, x_peer(i))

    def dr_flow(op):
        for i in range(1, 4):
            op(dop.at[lax.rem(y + i, 4)], dr.at[y], dr_send.at[i - 1], dr_recv, y_peer(i))

    def do_flow(op):
        for i in range(NH):
            h = lax.rem(s + 3 * r + i, NH)
            op(og.at[:, lanes(h)], dob.at[m, lax.rem(q, 2)], do_send.at[i], do_recv, (att_seq(h, r), x, half))

    def a_flow(op, mm):
        for k in range(2):
            op(a_out.at[mm, k], ab.at[lax.rem(mm, 4), :, lanes(att_h)], a_send, a_recv,
               (8 * (2 * r + k) + mm, x, att_w))

    def ay_flow(op):
        for i in range(1, 4):
            op(ab.at[y], ab.at[y], ay_send.at[i - 1], ay_recv, y_peer(i))

    def px_flow(op):
        for i in range(1, 4):
            op(pp.at[lax.rem(x + i, 4)], p1.at[x], px_send.at[i - 1], px_recv, x_peer(i))

    def p_flow(op):
        for i in range(4):
            op(ps4.at[i], pr.at[y], p_send.at[i], p_recv, (4 * z + x, i, r))

    def w0_flow(op):
        op(wgs, wg0, w0_send, w0_recv, sib_id)

    def w1_flow(op):
        for j, i in enumerate((1, 7)):
            op(wh.at[z_place(i)], wg1.at[j], w1_send.at[j], w1_recv.at[j], z_peer(i))
        for j, (block, i) in enumerate(((3, 1), (5, 7), (4, jnp.where(even, 2, 6)))):
            op(wh.at[z_place(block)], rl.at[j], rl_send.at[j], rl_recv.at[j], z_peer(i))

    def w2_flow(op):
        for j, i in enumerate((2, 6)):
            op(rs.at[j], wg1.at[2 + j], w1_send.at[2 + j], w1_recv.at[2 + j], z_peer(i))

    def ws_flow(op):
        op(wsum, wg_out.at[mine48], ws_send, ws_recv, sib_id)

    def c_flow(op):
        for i in range(1, 4):
            op(cpart, call.at[x], c_send.at[i - 1], c_recv, x_peer(i))

    def dq_flow(op, mm):
        for k in range(2):
            op(dqb.at[mm, k], dq_out.at[0, :, lanes(att_h)], dq_send, dq_recv,
               (8 * (2 * r + k) + mm, x, att_w))

    def dkv_flow(op, j):
        op(dkf.at[j], dkv.at[:, :, lanes(att_h)], dk_send, dk_recv, (16 * r + j, x, att_w))

    def fw_flow(op):
        part = kv.at[pl.ds(16 * r, 16), pl.ds(0, 144)]
        op(part, part, fw_send, fw_recv, sib_id)

    spill_copy = remote(gext.at[pl.ds(64, 8)], spill_in, sp_send, sp_recv, (s - 1, x, r))
    row_copy = remote(lrow, prow, lr_send, lr_recv, (s + 1, x, r))
    ex_copy = remote(acc.at[1 - r], sib, ex_send, ex_recv, sib_id)

    barrier = pltpu.get_barrier_semaphore()

    def greet(t):
        @pl.when(jnp.logical_not(same(t)))
        def _():
            pl.semaphore_signal(barrier, inc=1, device_id=t, device_id_type=MESH)

    for h in range(NH):
        for c in range(2):
            greet((att_seq(h, r), x, c))
    for i in range(1, 4):
        greet(y_peer(i))
        greet(x_peer(i))
    for i in (1, 2, 6, 7):
        greet(z_peer(i))
    for i in range(4):
        greet((4 * z + i, y, r))
        greet((4 * z + x, i, r))
    greet(sib_id)

    @pl.when(s > 0)
    def _():
        greet((s - 1, x, r))

    @pl.when(s < NS - 1)
    def _():
        greet((s + 1, x, r))

    @pl.when(is_att)
    def _():
        def one(j, _):
            greet((j, x, att_w))
            return 0

        lax.fori_loop(0, NS, one, 0)

    start_row = starts[...].astype(F32)
    before = lax.broadcasted_iota(jnp.int32, (NB, NB), 0) <= lax.broadcasted_iota(jnp.int32, (NB, NB), 1)
    tri = jnp.where(before, 1.0, 0.0).astype(BF16)
    rank = nn(jnp.broadcast_to(start_row, (16, NB)).astype(BF16), tri)[0:1] - 1.0
    count = jnp.sum(start_row, axis=1, keepdims=True)
    slot80 = lax.broadcasted_iota(jnp.int32, (80, NB), 0).astype(F32)
    want = jnp.where(slot80 < 64.0, slot80, jnp.where(slot80 == 64.0, -1.0, -2.0))
    sel = jnp.where(jnp.broadcast_to(rank, (80, NB)) == want, 1.0, 0.0)
    sel_s[...] = sel
    weight = sel * conf[...]
    w_hi = weight.astype(BF16)
    w_lo = (weight - w_hi.astype(F32)).astype(BF16)
    upstream = up[0]
    gext[...] = nn(w_hi, upstream) + nn(w_lo, upstream)
    for h in range(NH):
        cols = slice(h * HEAD_DIM, (h + 1) * HEAD_DIM)
        stage[h, 0:64] = k_in[0, :, cols]
        stage[h, 64:128] = v_in[0, :, cols]
        stage[h, 128:144] = jnp.broadcast_to(count, (16, HEAD_DIM)).astype(BF16)
        stage[h, 144:208] = q_in[0, :, cols]
    wq[z, mine48] = w_in[mine48]
    @pl.when(s == NS - 1)
    def _():
        spill_in[...] = jnp.zeros_like(spill_in)

    @pl.when(s == 0)
    def _():
        prow[...] = jnp.zeros_like(prow)

    partners = (
        12 + 3 + 3 + 4 + 8 + 1
        - jnp.where(x == y, 2, 0)
        + jnp.where(s > 0, 1, 0) + jnp.where(s < NS - 1, 1, 0)
        + jnp.where(is_att, jnp.where(att_w == r, 30, 32), 0)
    )
    pl.semaphore_wait(barrier, partners)

    @pl.when(s > 0)
    def _():
        spill_copy.start()

    kv_flow(send)
    wa_flow(start)

    place = lax.broadcasted_iota(jnp.int32, (1, 1024), 1)
    group, at = lax.div(place, 256), lax.rem(place, 256)
    source = jnp.where(at < 96, 96 * group + at, jnp.where(at < 192, 96 * group + 288 + at, -1))
    perm[...] = jnp.where(lax.broadcasted_iota(jnp.int32, (D, 1024), 0) == source, 1.0, 0.0).astype(BF16)
    packed = jnp.where(at < 192, 192 * group + at, -1)
    pack[...] = jnp.where(lax.broadcasted_iota(jnp.int32, (D, 1024), 0) == packed, 1.0, 0.0).astype(BF16)
    picked = sel[0:64] * start_row
    picked_t = picked.T.astype(BF16)
    grows[...] = nn(picked.astype(BF16), states[0])
    last = lax.broadcasted_iota(jnp.int32, (64, D), 0).astype(F32) == count - 1.0

    @pl.when(s < NS - 1)
    def _():
        spill_copy.wait_recv()

    group_grad = gext[0:64] + jnp.where(last, spill_in[0:1], 0.0)
    g_hi = group_grad.astype(BF16)
    spread = nn(g_hi, perm[...]).astype(BF16)
    for i in range(4):
        gp[i] = spread[:, 256 * i:256 * (i + 1)]
    g_flow(send)
    for j in (2, 3):
        landed(w_in.at[pl.ds(0, 48)], wa_recv.at[j])
    wb_flow(start)
    landed(gr, g_recv)
    gathered = jnp.concatenate([gr[0], gr[1], gr[2], gr[3]], axis=1)
    gq[x] = nt(gathered, pack[...]).astype(BF16)
    gx_flow(start)
    g_lo = (group_grad - g_hi.astype(F32)).astype(BF16)
    byte_grad[0] = (upstream.astype(F32) + nn(picked_t, g_hi) + nn(picked_t, g_lo)).astype(BF16)

    @pl.when(is_att)
    def _():
        landed(kv.at[pl.ds(16 * r, 16)], kv_recv)
        fw_flow(start)
        landed(kv.at[pl.ds(0, 16), pl.ds(0, 144)], fw_recv)
        kt[...] = kv[:, 0:64, :].reshape(2048, HEAD_DIM).T
        vt[...] = kv[:, 64:128, :].reshape(2048, HEAD_DIM).T
        lane = lax.broadcasted_iota(jnp.int32, (1, 128), 1).astype(F32)
        for p in range(16):
            c0 = kv[2 * p, 128:144, :].astype(F32)[0:1]
            c1 = kv[2 * p + 1, 128:144, :].astype(F32)[0:1]
            live = jnp.where(lane < 64.0, jnp.where(lane < c0, 1.0, 0.0), jnp.where(lane - 64.0 < c1, 1.0, 0.0))
            row = jnp.where(live > 0.0, lane + 128.0 * p, FAR_KEY)
            kkb[:, p * 128:(p + 1) * 128] = jnp.broadcast_to(row, (8, 128))

        def forward(step, _):
            i = lax.rem(step + att, 4)
            slot = lax.broadcasted_iota(jnp.int32, (64, 128), 0).astype(F32)
            places, queries = [], []
            for mm in range(2):
                for k in range(2):
                    block = 8 * (2 * r + k) + 2 * i + mm
                    cnt = kv[block, 128:144, :].astype(F32)[0:1]
                    base = (block * 64).astype(F32)
                    places.append(jnp.where(slot < cnt, slot + base, FAR_QUERY))
                    queries.append(kv[block, 144:208, :])
            place = jnp.concatenate(places, axis=0)
            place = jnp.concatenate([place] * 16, axis=1)
            scores = nn(jnp.concatenate(queries, axis=0), kt[...])
            scores = jnp.where(jnp.broadcast_to(kkb[0:1], (256, 2048)) <= place, scores, -jnp.inf)
            top = jnp.max(scores, axis=1, keepdims=True)
            attention = jnp.exp2((scores - top) * SCALE_LOG2E)
            total = jnp.sum(attention, axis=1, keepdims=True)
            rounded = attention.astype(BF16)
            probs[i] = rounded
            inverse = 1.0 / total
            inv[i] = jnp.broadcast_to(inverse, (256, HEAD_DIM))
            out = nn(rounded, kv[:, 64:128, :].reshape(2048, HEAD_DIM)) * inverse
            a_out[pl.ds(2 * i, 2)] = out.astype(BF16).reshape(2, 2, 64, HEAD_DIM)
            a_flow(send, 2 * i)
            a_flow(send, 2 * i + 1)
            return 0

        lax.fori_loop(0, 4, forward, 0)

    for j in (0, 1):
        landed(w_in.at[pl.ds(0, 48)], wa_recv.at[j])
    landed(wq.at[pl.ds(0, 3), pl.ds(0, 48)], wb_recv)
    wd_flow(start)
    landed(gq.at[pl.ds(0, 3)], gx_recv)
    landed(wq.at[:, pl.ds(0, 48)], wd_recv)

    g_all = gq[...].reshape(256, D)
    w_all = wq[...].reshape(D, D)
    dop[...] = nn(g_all, w_all).astype(BF16).reshape(4, 64, D)
    dr_flow(start)
    landed(w_in.at[pl.ds(0, 64)], a_recv)
    ay_flow(start)

    landed(dr.at[pl.ds(0, 3)], dr_recv)
    dr[y] = dop[y]
    og[...] = (dr[0].astype(F32) + dr[1].astype(F32) + dr[2].astype(F32) + dr[3].astype(F32)).astype(BF16)
    do_flow(send)

    landed(ab.at[pl.ds(0, 3)], ay_recv)
    a_all = ab[...].reshape(256, D)
    pp[...] = nt(a_all, wq[...].reshape(D, D)).astype(BF16).reshape(4, 64, D)
    px_flow(start)
    wgp[...] = nn(gq[...].reshape(256, D).T, a_all).reshape(8, 96, D)
    wgs[...] = wgp[:, pl.ds(pl.multiple_of(48 * (1 - r), 16), 48)].astype(BF16)
    w0_flow(start)


    @pl.when(is_att)
    def _():
        landed(dob, do_recv)
        acc[...] = jnp.zeros_like(acc)

        def backward(step, _):
            i = lax.rem(step + att, 4)
            queries = jnp.concatenate(
                [kv[8 * (2 * r + k) + 2 * i + mm, 144:208, :] for mm in range(2) for k in range(2)], axis=0)
            grad = dob[pl.ds(2 * i, 2)].reshape(256, HEAD_DIM).astype(F32)
            grad = (grad * inv[i]).astype(BF16)
            attended = a_out[pl.ds(2 * i, 2)].reshape(256, HEAD_DIM)
            dots = jnp.sum(grad.astype(F32) * attended.astype(F32), axis=1, keepdims=True)
            flow = nn(grad, vt[...])
            weights = probs[i]
            dscore = (weights.astype(F32) * (flow - dots)).astype(BF16)
            dq = nn(dscore, kv[:, 0:64, :].reshape(2048, HEAD_DIM)) * SCALE
            dqb[pl.ds(2 * i, 2)] = dq.astype(BF16).reshape(2, 2, 64, HEAD_DIM)
            dq_flow(send, 2 * i)
            dq_flow(send, 2 * i + 1)
            dk = nn(queries.T, dscore)
            dv = nn(grad.T, weights)
            for c in range(2):
                cols = slice(1024 * c, 1024 * (c + 1))
                acc[c, 0] += dk[:, cols]
                acc[c, 1] += dv[:, cols]
            return 0

        lax.fori_loop(0, 4, backward, 0)
        ex_copy.start()

    landed(wg0, w0_recv)
    wh[...] = (wgp[:, mine48] + wg0[...].astype(F32)).astype(BF16)
    w1_flow(start)

    landed(p1.at[pl.ds(0, 3)], px_recv)
    p1[x] = pp[x]
    summed = (p1[0].astype(F32) + p1[1].astype(F32) + p1[2].astype(F32) + p1[3].astype(F32)).astype(BF16)
    apart = nn(summed, pack[...]).astype(BF16)
    for i in range(4):
        ps4[i] = apart[:, 256 * i:256 * (i + 1)]
    p_flow(send)

    for j in range(3):
        landed(rl.at[j], rl_recv.at[j])
    far = rl[2].astype(F32)
    rs[0] = (wh[z_place(2)].astype(F32) + rl[0].astype(F32) + jnp.where(even, far, 0.0)).astype(BF16)
    rs[1] = (wh[z_place(6)].astype(F32) + rl[1].astype(F32) + jnp.where(even, 0.0, far)).astype(BF16)
    w2_flow(start)

    @pl.when(is_att)
    def _():
        ex_copy.wait_recv()
        dkf[:, 0] = ((acc[r, 0] + sib[0]) * SCALE).T.astype(BF16).reshape(16, 64, HEAD_DIM)
        dkf[:, 1] = (acc[r, 1] + sib[1]).T.astype(BF16).reshape(16, 64, HEAD_DIM)

        def out(step, _):
            dkv_flow(send, lax.rem(step + 3 * att, 16))
            return 0

        lax.fori_loop(0, 16, out, 0)
    landed(pr, p_recv)
    gathered = jnp.concatenate([pr[0], pr[1], pr[2], pr[3]], axis=1)
    group_out = (grows[...] + nt(gathered, perm[...])).astype(BF16)
    lrow[...] = jnp.broadcast_to(
        jnp.sum(jnp.where(last, group_out.astype(F32), 0.0), axis=0, keepdims=True), (16, D)
    ).astype(BF16)

    @pl.when(s < NS - 1)
    def _():
        row_copy.start()

    @pl.when(s > 0)
    def _():
        row_copy.wait_recv()

    rows = jnp.concatenate([group_out, prow[...]], axis=0)
    cross = nt(rows, up[0])
    part = jnp.sum(sel_s[...] * cross, axis=0, keepdims=True)
    cpart[...] = jnp.broadcast_to(part, (8, NB))
    call[x] = cpart[...]
    c_flow(start)
    total_w = wh[z].astype(F32)
    for j in range(4):
        landed(wg1.at[j], w1_recv.at[j])
        total_w = total_w + wg1[j].astype(F32)
    wsum[...] = total_w
    ws_flow(start)
    wg_out[mine48] = wsum[...]

    landed(call.at[pl.ds(0, 3)], c_recv)
    conf_grad[...] = (call[0] + call[1] + call[2] + call[3])[0:1]

    landed(wsum, ws_recv)
    kv_flow(sent)
    g_flow(sent)
    do_flow(sent)
    p_flow(sent)
    for flow in (wa_flow, wb_flow, wd_flow, gx_flow, dr_flow, ay_flow, px_flow, w0_flow, w1_flow, w2_flow, ws_flow, c_flow):
        flow(finish)

    @pl.when(s > 0)
    def _():
        spill_copy.wait_send()

    @pl.when(s < NS - 1)
    def _():
        row_copy.wait_send()

    @pl.when(is_att)
    def _():
        fw_flow(finish)
        ex_copy.wait_send()

        own = jnp.logical_and(att_w == r, half == r)
        for count_of, there in ((15, own), (16, jnp.logical_not(own))):
            @pl.when(there)
            def _(count_of=count_of):
                landed(kv.at[pl.ds(0, count_of), pl.ds(0, 64)], a_send)
                landed(kv.at[pl.ds(0, count_of), pl.ds(0, 64)], dq_send)
                landed(kv.at[pl.ds(0, count_of), pl.ds(0, 128)], dk_send)

    landed(dq_out, dq_recv)
    landed(dkv, dk_recv)
    dk_out[0] = dkv[0]
    dv_out[0] = dkv[1]


def hand_over(*refs):
    held, sems = refs[12:18], refs[18]
    come = [pltpu.make_async_copy(refs[i], held[i], sems.at[i]) for i in range(6)]
    leave = [pltpu.make_async_copy(held[i], refs[6 + i], sems.at[6 + i]) for i in range(6)]
    for copy in come:
        copy.start()
    for i in range(6):
        come[i].wait()
        leave[i].start()
    for copy in leave:
        copy.wait()


def local(byte_states, boundary, confidence, query_rows, key_rows, value_rows, out_weight, upstream):
    vmem = pl.BlockSpec(memory_space=pltpu.VMEM)
    dma = pltpu.SemaphoreType.DMA
    rows = jax.ShapeDtypeStruct((1, CAP, D), BF16)
    shapes = (
        jax.ShapeDtypeStruct((1, NB, D), BF16),
        jax.ShapeDtypeStruct((1, NB), F32),
        rows, rows, rows,
        jax.ShapeDtypeStruct((96, D), F32),
    )
    parts = pl.pallas_call(
        kernel,
        out_shape=shapes,
        in_specs=[vmem] * 8,
        out_specs=(vmem,) * 6,
        scratch_shapes=[
            pltpu.VMEM((NH, 208, 128), BF16),
            pltpu.VMEM((NS, 208, 128), BF16),
            pltpu.VMEM((8, 96, D), BF16),
            pltpu.VMEM((80, D), F32),
            pltpu.VMEM((8, D), F32),
            pltpu.VMEM((D, 1024), BF16),
            pltpu.VMEM((D, 1024), BF16),
            pltpu.VMEM((4, 64, 256), BF16),
            pltpu.VMEM((4, 64, 256), BF16),
            pltpu.VMEM((4, 64, D), BF16),
            pltpu.VMEM((4, 64, D), BF16),
            pltpu.VMEM((4, 64, D), BF16),
            pltpu.VMEM((64, D), BF16),
            pltpu.VMEM((8, 2, 64, 128), BF16),
            pltpu.VMEM((128, 2048), BF16),
            pltpu.VMEM((128, 2048), BF16),
            pltpu.VMEM((8, 2048), F32),
            pltpu.VMEM((4, 256, 2048), BF16),
            pltpu.VMEM((4, 256, 128), F32),
            pltpu.VMEM((8, 2, 64, 128), BF16),
            pltpu.VMEM((4, 64, D), BF16),
            pltpu.VMEM((4, 64, D), BF16),
            pltpu.VMEM((4, 64, D), BF16),
            pltpu.VMEM((4, 64, 256), BF16),
            pltpu.VMEM((4, 64, 256), BF16),
            pltpu.VMEM((8, 96, D), F32),
            pltpu.VMEM((8, 48, D), BF16),
            pltpu.VMEM((8, 48, D), BF16),
            pltpu.VMEM((8, 48, D), BF16),
            pltpu.VMEM((4, 48, D), BF16),
            pltpu.VMEM((3, 48, D), BF16),
            pltpu.VMEM((2, 48, D), BF16),
            pltpu.VMEM((48, D), F32),
            pltpu.VMEM((16, D), BF16),
            pltpu.VMEM((16, D), BF16),
            pltpu.VMEM((8, NB), F32),
            pltpu.VMEM((4, 8, NB), F32),
            pltpu.VMEM((8, 2, 64, 128), BF16),
            pltpu.VMEM((2, 2, 128, 1024), F32),
            pltpu.VMEM((2, 128, 1024), F32),
            pltpu.VMEM((16, 2, 64, 128), BF16),
            pltpu.VMEM((2, 64, D), BF16),
            pltpu.VMEM((80, NB), F32),
            pltpu.VMEM((64, D), F32),
            dma((6,)), dma,
            dma, dma,
            dma((4,)), dma((4,)),
            dma((3,)), dma,
            dma, dma,
            dma, dma,
            dma((4,)), dma,
            dma((3,)), dma,
            dma((3,)), dma,
            dma((6,)), dma,
            dma, dma,
            dma((3,)), dma,
            dma((3,)), dma,
            dma((4,)), dma,
            dma, dma,
            dma((4,)), dma((4,)),
            dma((3,)), dma((3,)),
            dma, dma,
            dma, dma,
            dma((3,)), dma,
            dma, dma,
            dma, dma,
            dma, dma,
        ],
        compiler_params=pltpu.CompilerParams(
            collective_id=0, has_side_effects=True, vmem_limit_bytes=56 * 1024 * 1024
        ),
        cost_estimate=pl.CostEstimate(flops=8_000_000_000, bytes_accessed=20_000_000, transcendentals=3_000_000),
    )(byte_states, boundary, confidence, query_rows, key_rows, value_rows, out_weight, upstream)
    whole = pl.BlockSpec(memory_space=pl.ANY)
    return pl.pallas_call(
        hand_over,
        out_shape=shapes,
        in_specs=[whole] * 6,
        out_specs=(whole,) * 6,
        scratch_shapes=[pltpu.VMEM(shape.shape, shape.dtype) for shape in shapes] + [dma((12,))],
        compiler_params=pltpu.CompilerParams(vmem_limit_bytes=60 * 1024 * 1024),
    )(*parts)


def solution(mesh):
    split = P("rep", "seq", "head")
    bytes_ = P("rep", "seq")
    return jax.shard_map(
        local,
        mesh=mesh,
        in_specs=(split, bytes_, bytes_, split, split, split, P("seq", "head"), split),
        out_specs=(split, bytes_, split, split, split, P("seq", "head")),
        check_vma=False,
    )
```

```python
import jax
import jax.numpy as jnp
from jax import lax
from jax.experimental import pallas as pl
from jax.experimental.pallas import tpu as pltpu
from jax.sharding import PartitionSpec as P

MESH = pl.DeviceIdType.MESH
F32, BF16 = jnp.float32, jnp.bfloat16

HEAD_DIM = 128
NS = 32
NH = 6
D = 768
CAP = 64
NB = 256
SCALE = HEAD_DIM ** -0.5
SCALE_LOG2E = SCALE * 1.4426950408889634
FAR_QUERY = 4096.0
FAR_KEY = 8192.0


def att_seq(h, w):
    return lax.div((2 * h + w) * 8, 3)


def nt(a, b):
    return lax.dot_general(a, b, (((1,), (1,)), ((), ())), preferred_element_type=F32)


def nn(a, b):
    return jnp.dot(a, b, preferred_element_type=F32)


def kernel(
    states, starts, conf, q_in, k_in, v_in, w_in, up,
    byte_grad, conf_grad, dq_out, dk_out, dv_out, wg_out,
    stage, kv, wq, gext, spill_in, perm, pack, gp, gr, gq, dop, dr, og, dob,
    kt, vt, kkb, probs, inv, a_out, ab, pp, p1, ps4, pr, wgp, wgs, wg0, wh, wg1, rl, rs, wsum,
    lrow, prow, cpart, call, dqb, acc, sib, dkf, dkv, sel_s, grows,
    kv_send, kv_recv, fw_send, fw_recv, wa_send, wa_recv, wb_send, wb_recv, wd_send, wd_recv,
    sp_send, sp_recv, g_send, g_recv, gx_send, gx_recv, dr_send, dr_recv,
    do_send, do_recv, a_send, a_recv, ay_send, ay_recv, px_send, px_recv, p_send, p_recv,
    w0_send, w0_recv, w1_send, w1_recv, rl_send, rl_recv, ws_send, ws_recv,
    lr_send, lr_recv, c_send, c_recv, dq_send, dq_recv, dk_send, dk_recv,
    ex_send, ex_recv,
):
    s = lax.axis_index("seq")
    x = lax.axis_index("head")
    r = lax.axis_index("rep")
    q = lax.div(s, 8)
    m = lax.rem(s, 8)
    z = lax.div(s, 4)
    y = lax.rem(m, 4)
    half = lax.div(q, 2)
    att = lax.div(3 * s + 7, 8)
    is_att = jnp.logical_and(lax.div(att * 8, 3) == s, att < 12)
    att_h = lax.div(att, 2)
    att_w = lax.rem(att, 2)

    def same(t):
        return jnp.logical_and(jnp.logical_and(t[0] == s, t[1] == x), t[2] == r)

    def send(src, dst, ssem, rsem, t):
        mine = same(t)

        @pl.when(jnp.logical_not(mine))
        def _():
            pltpu.make_async_remote_copy(src, dst, ssem, rsem, device_id=t, device_id_type=MESH).start()

        @pl.when(mine)
        def _():
            pltpu.make_async_copy(src, dst, rsem).start()

    def sent(src, dst, ssem, rsem, t):
        @pl.when(jnp.logical_not(same(t)))
        def _():
            pltpu.make_async_remote_copy(src, dst, ssem, rsem, device_id=t, device_id_type=MESH).wait_send()

    def landed(ref, rsem):
        pltpu.make_async_copy(ref, ref, rsem).wait()

    def remote(src, dst, ssem, rsem, t):
        return pltpu.make_async_remote_copy(src, dst, ssem, rsem, device_id=t, device_id_type=MESH)

    def start(*a):
        remote(*a).start()

    def finish(*a):
        remote(*a).wait_send()

    def lanes(h):
        return pl.ds(h * HEAD_DIM if isinstance(h, int) else pl.multiple_of(h * HEAD_DIM, HEAD_DIM), HEAD_DIM)

    mine48 = pl.ds(pl.multiple_of(48 * r, 16), 48)
    sib_id = (s, x, 1 - r)

    def y_peer(i):
        return (s - y + lax.rem(y + i, 4), x, r)

    def z_place(i):
        return lax.rem(z + i, 8)

    def z_peer(i):
        return (4 * z_place(i) + y, x, r)

    def x_peer(i):
        return (s, lax.rem(x + i, 4), r)

    def kv_flow(op):
        for i in range(NH):
            h = lax.rem(s + 3 * r + i, NH)
            op(stage.at[h], kv.at[s], kv_send.at[i], kv_recv, (att_seq(h, r), x, half))

    even = lax.rem(z, 2) == 0

    def wa_flow(op):
        for j, i in enumerate((1, 7, 2, 6)):
            op(w_in.at[mine48], wq.at[z, mine48], wa_send.at[j], wa_recv.at[j], z_peer(i))

    def wb_flow(op):
        for j, (block, i) in enumerate(((6, 1), (2, 7), (jnp.where(even, 6, 2), jnp.where(even, 2, 6)))):
            part = wq.at[z_place(block), mine48]
            op(part, part, wb_send.at[j], wb_recv, z_peer(i))

    def wd_flow(op):
        op(wq.at[:, mine48], wq.at[:, mine48], wd_send, wd_recv, sib_id)

    def g_flow(op):
        for i in range(4):
            op(gp.at[i], gr.at[x], g_send.at[i], g_recv, (4 * z + i, y, r))

    def gx_flow(op):
        for i in range(1, 4):
            op(gq.at[x], gq.at[x], gx_send.at[i - 1], gx_recv, x_peer(i))

    def dr_flow(op):
        for i in range(1, 4):
            op(dop.at[lax.rem(y + i, 4)], dr.at[y], dr_send.at[i - 1], dr_recv, y_peer(i))

    def do_flow(op):
        for i in range(NH):
            h = lax.rem(s + 3 * r + i, NH)
            op(og.at[:, lanes(h)], dob.at[m, lax.rem(q, 2)], do_send.at[i], do_recv, (att_seq(h, r), x, half))

    def a_flow(op, mm):
        for k in range(2):
            op(a_out.at[mm, k], ab.at[lax.rem(mm, 4), :, lanes(att_h)], a_send, a_recv,
               (8 * (2 * r + k) + mm, x, att_w))

    def ay_flow(op):
        for i in range(1, 4):
            op(ab.at[y], ab.at[y], ay_send.at[i - 1], ay_recv, y_peer(i))

    def px_flow(op):
        for i in range(1, 4):
            op(pp.at[lax.rem(x + i, 4)], p1.at[x], px_send.at[i - 1], px_recv, x_peer(i))

    def p_flow(op):
        for i in range(4):
            op(ps4.at[i], pr.at[y], p_send.at[i], p_recv, (4 * z + x, i, r))

    def w0_flow(op):
        op(wgs, wg0, w0_send, w0_recv, sib_id)

    def w1_flow(op):
        for j, i in enumerate((1, 7)):
            op(wh.at[z_place(i)], wg1.at[j], w1_send.at[j], w1_recv.at[j], z_peer(i))
        for j, (block, i) in enumerate(((3, 1), (5, 7), (4, jnp.where(even, 2, 6)))):
            op(wh.at[z_place(block)], rl.at[j], rl_send.at[j], rl_recv.at[j], z_peer(i))

    def w2_flow(op):
        for j, i in enumerate((2, 6)):
            op(rs.at[j], wg1.at[2 + j], w1_send.at[2 + j], w1_recv.at[2 + j], z_peer(i))

    def ws_flow(op):
        op(wsum, wg_out.at[mine48], ws_send, ws_recv, sib_id)

    def c_flow(op):
        for i in range(1, 4):
            op(cpart, call.at[x], c_send.at[i - 1], c_recv, x_peer(i))

    def dq_flow(op, mm):
        for k in range(2):
            op(dqb.at[mm, k], dq_out.at[0, :, lanes(att_h)], dq_send, dq_recv,
               (8 * (2 * r + k) + mm, x, att_w))

    def dkv_flow(op, j):
        op(dkf.at[j], dkv.at[:, :, lanes(att_h)], dk_send, dk_recv, (16 * r + j, x, att_w))

    def fw_flow(op):
        part = kv.at[pl.ds(16 * r, 16), pl.ds(0, 144)]
        op(part, part, fw_send, fw_recv, sib_id)

    spill_copy = remote(gext.at[pl.ds(64, 8)], spill_in, sp_send, sp_recv, (s - 1, x, r))
    row_copy = remote(lrow, prow, lr_send, lr_recv, (s + 1, x, r))
    ex_copy = remote(acc.at[1 - r], sib, ex_send, ex_recv, sib_id)

    barrier = pltpu.get_barrier_semaphore()

    def greet(t):
        @pl.when(jnp.logical_not(same(t)))
        def _():
            pl.semaphore_signal(barrier, inc=1, device_id=t, device_id_type=MESH)

    for h in range(NH):
        for c in range(2):
            greet((att_seq(h, r), x, c))
    for i in range(1, 4):
        greet(y_peer(i))
        greet(x_peer(i))
    for i in (1, 2, 6, 7):
        greet(z_peer(i))
    for i in range(4):
        greet((4 * z + i, y, r))
        greet((4 * z + x, i, r))
    greet(sib_id)

    @pl.when(s > 0)
    def _():
        greet((s - 1, x, r))

    @pl.when(s < NS - 1)
    def _():
        greet((s + 1, x, r))

    @pl.when(is_att)
    def _():
        def one(j, _):
            greet((j, x, att_w))
            return 0

        lax.fori_loop(0, NS, one, 0)

    start_row = starts[...].astype(F32)
    before = lax.broadcasted_iota(jnp.int32, (NB, NB), 0) <= lax.broadcasted_iota(jnp.int32, (NB, NB), 1)
    tri = jnp.where(before, 1.0, 0.0).astype(BF16)
    rank = nn(jnp.broadcast_to(start_row, (16, NB)).astype(BF16), tri)[0:1] - 1.0
    count = jnp.sum(start_row, axis=1, keepdims=True)
    slot80 = lax.broadcasted_iota(jnp.int32, (80, NB), 0).astype(F32)
    want = jnp.where(slot80 < 64.0, slot80, jnp.where(slot80 == 64.0, -1.0, -2.0))
    sel = jnp.where(jnp.broadcast_to(rank, (80, NB)) == want, 1.0, 0.0)
    sel_s[...] = sel
    weight = sel * conf[...]
    w_hi = weight.astype(BF16)
    w_lo = (weight - w_hi.astype(F32)).astype(BF16)
    upstream = up[0]
    gext[...] = nn(w_hi, upstream) + nn(w_lo, upstream)
    for h in range(NH):
        cols = slice(h * HEAD_DIM, (h + 1) * HEAD_DIM)
        stage[h, 0:64] = k_in[0, :, cols]
        stage[h, 64:128] = v_in[0, :, cols]
        stage[h, 128:144] = jnp.broadcast_to(count, (16, HEAD_DIM)).astype(BF16)
        stage[h, 144:208] = q_in[0, :, cols]
    wq[z, mine48] = w_in[mine48]
    @pl.when(s == NS - 1)
    def _():
        spill_in[...] = jnp.zeros_like(spill_in)

    @pl.when(s == 0)
    def _():
        prow[...] = jnp.zeros_like(prow)

    partners = (
        12 + 3 + 3 + 4 + 8 + 1
        - jnp.where(x == y, 2, 0)
        + jnp.where(s > 0, 1, 0) + jnp.where(s < NS - 1, 1, 0)
        + jnp.where(is_att, jnp.where(att_w == r, 30, 32), 0)
    )
    pl.semaphore_wait(barrier, partners)

    @pl.when(s > 0)
    def _():
        spill_copy.start()

    kv_flow(send)
    wa_flow(start)

    place = lax.broadcasted_iota(jnp.int32, (1, 1024), 1)
    group, at = lax.div(place, 256), lax.rem(place, 256)
    source = jnp.where(at < 96, 96 * group + at, jnp.where(at < 192, 96 * group + 288 + at, -1))
    perm[...] = jnp.where(lax.broadcasted_iota(jnp.int32, (D, 1024), 0) == source, 1.0, 0.0).astype(BF16)
    packed = jnp.where(at < 192, 192 * group + at, -1)
    pack[...] = jnp.where(lax.broadcasted_iota(jnp.int32, (D, 1024), 0) == packed, 1.0, 0.0).astype(BF16)
    picked = sel[0:64] * start_row
    picked_t = picked.T.astype(BF16)
    grows[...] = nn(picked.astype(BF16), states[0])
    last = lax.broadcasted_iota(jnp.int32, (64, D), 0).astype(F32) == count - 1.0

    @pl.when(s < NS - 1)
    def _():
        spill_copy.wait_recv()

    group_grad = gext[0:64] + jnp.where(last, spill_in[0:1], 0.0)
    g_hi = group_grad.astype(BF16)
    spread = nn(g_hi, perm[...]).astype(BF16)
    for i in range(4):
        gp[i] = spread[:, 256 * i:256 * (i + 1)]
    g_flow(send)
    for j in (2, 3):
        landed(w_in.at[pl.ds(0, 48)], wa_recv.at[j])
    wb_flow(start)
    landed(gr, g_recv)
    gathered = jnp.concatenate([gr[0], gr[1], gr[2], gr[3]], axis=1)
    gq[x] = nt(gathered, pack[...]).astype(BF16)
    gx_flow(start)
    g_lo = (group_grad - g_hi.astype(F32)).astype(BF16)
    byte_grad[0] = (upstream.astype(F32) + nn(picked_t, g_hi) + nn(picked_t, g_lo)).astype(BF16)

    @pl.when(is_att)
    def _():
        landed(kv.at[pl.ds(16 * r, 16)], kv_recv)
        fw_flow(start)
        landed(kv.at[pl.ds(0, 16), pl.ds(0, 144)], fw_recv)
        kt[...] = kv[:, 0:64, :].reshape(2048, HEAD_DIM).T
        vt[...] = kv[:, 64:128, :].reshape(2048, HEAD_DIM).T
        lane = lax.broadcasted_iota(jnp.int32, (1, 128), 1).astype(F32)
        for p in range(16):
            c0 = kv[2 * p, 128:144, :].astype(F32)[0:1]
            c1 = kv[2 * p + 1, 128:144, :].astype(F32)[0:1]
            live = jnp.where(lane < 64.0, jnp.where(lane < c0, 1.0, 0.0), jnp.where(lane - 64.0 < c1, 1.0, 0.0))
            row = jnp.where(live > 0.0, lane + 128.0 * p, FAR_KEY)
            kkb[:, p * 128:(p + 1) * 128] = jnp.broadcast_to(row, (8, 128))

        def forward(step, _):
            i = lax.rem(step + att, 4)
            slot = lax.broadcasted_iota(jnp.int32, (64, 128), 0).astype(F32)
            places, queries = [], []
            for mm in range(2):
                for k in range(2):
                    block = 8 * (2 * r + k) + 2 * i + mm
                    cnt = kv[block, 128:144, :].astype(F32)[0:1]
                    base = (block * 64).astype(F32)
                    places.append(jnp.where(slot < cnt, slot + base, FAR_QUERY))
                    queries.append(kv[block, 144:208, :])
            place = jnp.concatenate(places, axis=0)
            place = jnp.concatenate([place] * 16, axis=1)
            scores = nn(jnp.concatenate(queries, axis=0), kt[...])
            scores = jnp.where(jnp.broadcast_to(kkb[0:1], (256, 2048)) <= place, scores, -jnp.inf)
            top = jnp.max(scores, axis=1, keepdims=True)
            attention = jnp.exp2((scores - top) * SCALE_LOG2E)
            total = jnp.sum(attention, axis=1, keepdims=True)
            rounded = attention.astype(BF16)
            probs[i] = rounded
            inverse = 1.0 / total
            inv[i] = jnp.broadcast_to(inverse, (256, HEAD_DIM))
            out = nn(rounded, kv[:, 64:128, :].reshape(2048, HEAD_DIM)) * inverse
            a_out[pl.ds(2 * i, 2)] = out.astype(BF16).reshape(2, 2, 64, HEAD_DIM)
            a_flow(send, 2 * i)
            a_flow(send, 2 * i + 1)
            return 0

        lax.fori_loop(0, 4, forward, 0)

    for j in (0, 1):
        landed(w_in.at[pl.ds(0, 48)], wa_recv.at[j])
    landed(wq.at[pl.ds(0, 3), pl.ds(0, 48)], wb_recv)
    wd_flow(start)
    landed(gq.at[pl.ds(0, 3)], gx_recv)
    landed(wq.at[:, pl.ds(0, 48)], wd_recv)

    g_all = gq[...].reshape(256, D)
    w_all = wq[...].reshape(D, D)
    dop[...] = nn(g_all, w_all).astype(BF16).reshape(4, 64, D)
    dr_flow(start)
    landed(w_in.at[pl.ds(0, 64)], a_recv)
    ay_flow(start)

    landed(dr.at[pl.ds(0, 3)], dr_recv)
    dr[y] = dop[y]
    og[...] = (dr[0].astype(F32) + dr[1].astype(F32) + dr[2].astype(F32) + dr[3].astype(F32)).astype(BF16)
    do_flow(send)

    landed(ab.at[pl.ds(0, 3)], ay_recv)
    a_all = ab[...].reshape(256, D)
    pp[...] = nt(a_all, wq[...].reshape(D, D)).astype(BF16).reshape(4, 64, D)
    px_flow(start)
    wgp[...] = nn(gq[...].reshape(256, D).T, a_all).reshape(8, 96, D)
    wgs[...] = wgp[:, pl.ds(pl.multiple_of(48 * (1 - r), 16), 48)].astype(BF16)
    w0_flow(start)


    @pl.when(is_att)
    def _():
        landed(dob, do_recv)
        acc[...] = jnp.zeros_like(acc)

        def backward(step, _):
            i = lax.rem(step + att, 4)
            queries = jnp.concatenate(
                [kv[8 * (2 * r + k) + 2 * i + mm, 144:208, :] for mm in range(2) for k in range(2)], axis=0)
            grad = dob[pl.ds(2 * i, 2)].reshape(256, HEAD_DIM).astype(F32)
            grad = (grad * inv[i]).astype(BF16)
            attended = a_out[pl.ds(2 * i, 2)].reshape(256, HEAD_DIM)
            dots = jnp.sum(grad.astype(F32) * attended.astype(F32), axis=1, keepdims=True)
            flow = nn(grad, vt[...])
            weights = probs[i]
            dscore = (weights.astype(F32) * (flow - dots)).astype(BF16)
            dq = nn(dscore, kv[:, 0:64, :].reshape(2048, HEAD_DIM)) * SCALE
            dqb[pl.ds(2 * i, 2)] = dq.astype(BF16).reshape(2, 2, 64, HEAD_DIM)
            dq_flow(send, 2 * i)
            dq_flow(send, 2 * i + 1)
            dk = nn(queries.T, dscore)
            dv = nn(grad.T, weights)
            for c in range(2):
                cols = slice(1024 * c, 1024 * (c + 1))
                acc[c, 0] += dk[:, cols]
                acc[c, 1] += dv[:, cols]
            return 0

        lax.fori_loop(0, 4, backward, 0)
        ex_copy.start()

    landed(wg0, w0_recv)
    wh[...] = (wgp[:, mine48] + wg0[...].astype(F32)).astype(BF16)
    w1_flow(start)

    landed(p1.at[pl.ds(0, 3)], px_recv)
    p1[x] = pp[x]
    summed = (p1[0].astype(F32) + p1[1].astype(F32) + p1[2].astype(F32) + p1[3].astype(F32)).astype(BF16)
    apart = nn(summed, pack[...]).astype(BF16)
    for i in range(4):
        ps4[i] = apart[:, 256 * i:256 * (i + 1)]
    p_flow(send)

    for j in range(3):
        landed(rl.at[j], rl_recv.at[j])
    far = rl[2].astype(F32)
    rs[0] = (wh[z_place(2)].astype(F32) + rl[0].astype(F32) + jnp.where(even, far, 0.0)).astype(BF16)
    rs[1] = (wh[z_place(6)].astype(F32) + rl[1].astype(F32) + jnp.where(even, 0.0, far)).astype(BF16)
    w2_flow(start)

    landed(pr, p_recv)
    gathered = jnp.concatenate([pr[0], pr[1], pr[2], pr[3]], axis=1)
    group_out = (grows[...] + nt(gathered, perm[...])).astype(BF16)
    lrow[...] = jnp.broadcast_to(
        jnp.sum(jnp.where(last, group_out.astype(F32), 0.0), axis=0, keepdims=True), (16, D)
    ).astype(BF16)

    @pl.when(s < NS - 1)
    def _():
        row_copy.start()

    @pl.when(is_att)
    def _():
        ex_copy.wait_recv()
        dkf[:, 0] = ((acc[r, 0] + sib[0]) * SCALE).T.astype(BF16).reshape(16, 64, HEAD_DIM)
        dkf[:, 1] = (acc[r, 1] + sib[1]).T.astype(BF16).reshape(16, 64, HEAD_DIM)

        def out(step, _):
            dkv_flow(send, lax.rem(step + 3 * att, 16))
            return 0

        lax.fori_loop(0, 16, out, 0)
    @pl.when(s > 0)
    def _():
        row_copy.wait_recv()

    rows = jnp.concatenate([group_out, prow[...]], axis=0)
    cross = nt(rows, up[0])
    part = jnp.sum(sel_s[...] * cross, axis=0, keepdims=True)
    cpart[...] = jnp.broadcast_to(part, (8, NB))
    call[x] = cpart[...]
    c_flow(start)
    total_w = wh[z].astype(F32)
    for j in range(4):
        landed(wg1.at[j], w1_recv.at[j])
        total_w = total_w + wg1[j].astype(F32)
    wsum[...] = total_w
    ws_flow(start)
    wg_out[mine48] = wsum[...]

    landed(call.at[pl.ds(0, 3)], c_recv)
    conf_grad[...] = (call[0] + call[1] + call[2] + call[3])[0:1]

    landed(wsum, ws_recv)
    kv_flow(sent)
    g_flow(sent)
    do_flow(sent)
    p_flow(sent)
    for flow in (wa_flow, wb_flow, wd_flow, gx_flow, dr_flow, ay_flow, px_flow, w0_flow, w1_flow, w2_flow, ws_flow, c_flow):
        flow(finish)

    @pl.when(s > 0)
    def _():
        spill_copy.wait_send()

    @pl.when(s < NS - 1)
    def _():
        row_copy.wait_send()

    @pl.when(is_att)
    def _():
        fw_flow(finish)
        ex_copy.wait_send()

        own = jnp.logical_and(att_w == r, half == r)
        for count_of, there in ((15, own), (16, jnp.logical_not(own))):
            @pl.when(there)
            def _(count_of=count_of):
                landed(kv.at[pl.ds(0, count_of), pl.ds(0, 64)], a_send)
                landed(kv.at[pl.ds(0, count_of), pl.ds(0, 64)], dq_send)
                landed(kv.at[pl.ds(0, count_of), pl.ds(0, 128)], dk_send)

    landed(dq_out, dq_recv)
    landed(dkv, dk_recv)
    dk_out[0] = dkv[0]
    dv_out[0] = dkv[1]


def hand_over(*refs):
    held, sems = refs[12:18], refs[18]
    come = [pltpu.make_async_copy(refs[i], held[i], sems.at[i]) for i in range(6)]
    leave = [pltpu.make_async_copy(held[i], refs[6 + i], sems.at[6 + i]) for i in range(6)]
    for copy in come:
        copy.start()
    for i in range(6):
        come[i].wait()
        leave[i].start()
    for copy in leave:
        copy.wait()


def local(byte_states, boundary, confidence, query_rows, key_rows, value_rows, out_weight, upstream):
    vmem = pl.BlockSpec(memory_space=pltpu.VMEM)
    dma = pltpu.SemaphoreType.DMA
    rows = jax.ShapeDtypeStruct((1, CAP, D), BF16)
    shapes = (
        jax.ShapeDtypeStruct((1, NB, D), BF16),
        jax.ShapeDtypeStruct((1, NB), F32),
        rows, rows, rows,
        jax.ShapeDtypeStruct((96, D), F32),
    )
    parts = pl.pallas_call(
        kernel,
        out_shape=shapes,
        in_specs=[vmem] * 8,
        out_specs=(vmem,) * 6,
        scratch_shapes=[
            pltpu.VMEM((NH, 208, 128), BF16),
            pltpu.VMEM((NS, 208, 128), BF16),
            pltpu.VMEM((8, 96, D), BF16),
            pltpu.VMEM((80, D), F32),
            pltpu.VMEM((8, D), F32),
            pltpu.VMEM((D, 1024), BF16),
            pltpu.VMEM((D, 1024), BF16),
            pltpu.VMEM((4, 64, 256), BF16),
            pltpu.VMEM((4, 64, 256), BF16),
            pltpu.VMEM((4, 64, D), BF16),
            pltpu.VMEM((4, 64, D), BF16),
            pltpu.VMEM((4, 64, D), BF16),
            pltpu.VMEM((64, D), BF16),
            pltpu.VMEM((8, 2, 64, 128), BF16),
            pltpu.VMEM((128, 2048), BF16),
            pltpu.VMEM((128, 2048), BF16),
            pltpu.VMEM((8, 2048), F32),
            pltpu.VMEM((4, 256, 2048), BF16),
            pltpu.VMEM((4, 256, 128), F32),
            pltpu.VMEM((8, 2, 64, 128), BF16),
            pltpu.VMEM((4, 64, D), BF16),
            pltpu.VMEM((4, 64, D), BF16),
            pltpu.VMEM((4, 64, D), BF16),
            pltpu.VMEM((4, 64, 256), BF16),
            pltpu.VMEM((4, 64, 256), BF16),
            pltpu.VMEM((8, 96, D), F32),
            pltpu.VMEM((8, 48, D), BF16),
            pltpu.VMEM((8, 48, D), BF16),
            pltpu.VMEM((8, 48, D), BF16),
            pltpu.VMEM((4, 48, D), BF16),
            pltpu.VMEM((3, 48, D), BF16),
            pltpu.VMEM((2, 48, D), BF16),
            pltpu.VMEM((48, D), F32),
            pltpu.VMEM((16, D), BF16),
            pltpu.VMEM((16, D), BF16),
            pltpu.VMEM((8, NB), F32),
            pltpu.VMEM((4, 8, NB), F32),
            pltpu.VMEM((8, 2, 64, 128), BF16),
            pltpu.VMEM((2, 2, 128, 1024), F32),
            pltpu.VMEM((2, 128, 1024), F32),
            pltpu.VMEM((16, 2, 64, 128), BF16),
            pltpu.VMEM((2, 64, D), BF16),
            pltpu.VMEM((80, NB), F32),
            pltpu.VMEM((64, D), F32),
            dma((6,)), dma,
            dma, dma,
            dma((4,)), dma((4,)),
            dma((3,)), dma,
            dma, dma,
            dma, dma,
            dma((4,)), dma,
            dma((3,)), dma,
            dma((3,)), dma,
            dma((6,)), dma,
            dma, dma,
            dma((3,)), dma,
            dma((3,)), dma,
            dma((4,)), dma,
            dma, dma,
            dma((4,)), dma((4,)),
            dma((3,)), dma((3,)),
            dma, dma,
            dma, dma,
            dma((3,)), dma,
            dma, dma,
            dma, dma,
            dma, dma,
        ],
        compiler_params=pltpu.CompilerParams(
            collective_id=0, has_side_effects=True, vmem_limit_bytes=56 * 1024 * 1024
        ),
        cost_estimate=pl.CostEstimate(flops=8_000_000_000, bytes_accessed=20_000_000, transcendentals=3_000_000),
    )(byte_states, boundary, confidence, query_rows, key_rows, value_rows, out_weight, upstream)
    whole = pl.BlockSpec(memory_space=pl.ANY)
    return pl.pallas_call(
        hand_over,
        out_shape=shapes,
        in_specs=[whole] * 6,
        out_specs=(whole,) * 6,
        scratch_shapes=[pltpu.VMEM(shape.shape, shape.dtype) for shape in shapes] + [dma((12,))],
        compiler_params=pltpu.CompilerParams(vmem_limit_bytes=60 * 1024 * 1024),
    )(*parts)


def solution(mesh):
    split = P("rep", "seq", "head")
    bytes_ = P("rep", "seq")
    return jax.shard_map(
        local,
        mesh=mesh,
        in_specs=(split, bytes_, bytes_, split, split, split, P("seq", "head"), split),
        out_specs=(split, bytes_, split, split, split, P("seq", "head")),
        check_vma=False,
    )
```
